256 devices in a mesh: section: 8 (over z_hi, core), ctx: 8 (over z_lo, x), tp: 4 (over y).
Axes of the slice: x: 4, y: 4, z: 8 (z_hi: 4, z_lo: 2; z = z_hi * 2 + z_lo), core: 2. Of those that a mesh axis runs over, the one named last changes fastest.
Arguments:
- fwd_input: bfloat16 [8, 1024, 6144], P('section', 'ctx', 'tp'), may hold values from -6 to 6
- grad_out: bfloat16 [8, 1024, 6144], P('section', 'ctx', 'tp'), may hold values from -6 to 6
- w_qkv: bfloat16 [8, 3, 6144, 32, 128], P('section', None, 'tp', 'ctx'), may hold values from -1 to 1
- w_out: bfloat16 [8, 32, 128, 6144], P('section', 'ctx', None, 'tp'), may hold values from -0.5 to 0.5
- saved_qkv: bfloat16 [8, 3, 1024, 32, 128], P('section', None, None, ('ctx', 'tp')), may hold values from -6 to 6
- rand_blocks: int32 [8, 32, 16, 3], P('section', ('ctx', 'tp')), may hold values from 0 to 15
Outputs:
- fwd_next: bfloat16 [8, 1024, 6144], P('section', 'ctx', 'tp')
- grad_prev: bfloat16 [8, 1024, 6144], P('section', 'ctx', 'tp')
The draws below stay inside these ranges and needn't reach their ends.
Inputs may be any that keep to these rules, and one draw needn't show every extreme that they name: `rand_blocks`: key block indices.
All inputs are finite; a program needn't handle non-finite values.
Results may differ from the reference program's by a relative error of at most 0.025.
Values may be sent and summed in bfloat16 or wider, within the bound.
A program may use at most 128 MiB of HBM per device.

```python
import math
import jax
import jax.numpy as jnp
from jax import lax

D = 6144
H = 32
DH = 128
BLOCK = 64
GLOB = 2
NRAND = 3
SEQ = 1024
SECTIONS = 8
NBLK = 16
DT = 1536
HC = 4
N_CTX = 8
N_TP = 4


def draw_fwd_input(key, part):
    shape = (SECTIONS, SEQ, D)
    key = jax.random.fold_in(key, 11)
    return jax.random.truncated_normal(key, -6.0, 6.0, shape, jnp.float32).astype(jnp.bfloat16)


def draw_w_qkv(key, part):
    shape = (SECTIONS, 3, D, H, DH)
    key = jax.random.fold_in(key, 21)
    return (jax.random.truncated_normal(key, -6.0, 6.0, shape, jnp.float32) * D ** (-0.5)).astype(jnp.bfloat16)


def draw_saved_qkv(key, part):
    key = jax.random.fold_in(key, 3)
    shape = (SECTIONS, 3, SEQ, H, DH)
    return jax.random.truncated_normal(key, -6.0, 6.0, shape, jnp.float32).astype(jnp.bfloat16)


def touch_ends(drawn, stream_key, smallest, high):
    longest = drawn.shape.index(max(drawn.shape))
    spots = []
    for shift in (0, 1):
        where = [jax.random.randint(jax.random.fold_in(stream_key, axis), (), 0, length) for axis, length in enumerate(drawn.shape)]
        where[longest] = (where[longest] + shift) % drawn.shape[longest]
        spots.append(tuple(where))
    return drawn.at[spots[0]].set(smallest).at[spots[1]].set(high)


def levels(stream_key, shape, pieces, low, high):
    level = 1.0
    for dim, blocks in pieces:
        steps = jax.random.uniform(jax.random.fold_in(jax.random.fold_in(stream_key, 6), dim), (blocks,), jnp.float32, low / len(pieces), high / len(pieces))
        level = level * jnp.repeat(jnp.exp(steps), shape[dim] // blocks).reshape((-1,) + (1,) * (len(shape) - 1 - dim))
    return level


def noise(rng, extent, spread, most, shards=(), kind=jnp.bfloat16):
    entries = jax.random.normal(rng, extent, jnp.float32) * spread
    if len(shards) > 0:
        entries = levels(rng, extent, shards, -0.22, 0.18) * entries
    return jnp.clip(entries, min=-most, max=most).astype(kind)


def setup_inputs(seed: int = 0) -> dict:
    arg_keys = jax.random.split(jax.random.key(seed), 7)
    fwd_input = draw_fwd_input(jax.random.fold_in(arg_keys[6], 71), 0)
    grad_out = noise(arg_keys[1], (SECTIONS, SEQ, D), 1.0, 6.0, ((0, 8), (1, 8), (2, 4)))
    w_qkv = draw_w_qkv(jax.random.fold_in(arg_keys[6], 71), 0)
    w_out = noise(arg_keys[3], (SECTIONS, H, DH, D), DH ** -0.5, 0.5, ((0, 8), (1, 8), (3, 4)))
    saved_qkv = draw_saved_qkv(jax.random.fold_in(arg_keys[6], 71), 0)
    rand_blocks = touch_ends(jax.random.randint(arg_keys[5], (SECTIONS, H, NBLK, NRAND), 0, NBLK), jax.random.fold_in(arg_keys[5], 1), 0, NBLK - 1).astype(jnp.int32)
    return dict(fwd_input=fwd_input, grad_out=grad_out, w_qkv=w_qkv, w_out=w_out, saved_qkv=saved_qkv, rand_blocks=rand_blocks)


def rounded(value):
    return lax.optimization_barrier(value.astype(jnp.bfloat16)).astype(jnp.float32)

def pattern_lists(rand_rows, num_blocks):
    row_ids = lax.broadcasted_iota(jnp.int32, (num_blocks, 3), 0)
    offsets = lax.broadcasted_iota(jnp.int32, (num_blocks, 3), 1) - 1
    near_blocks = (row_ids + offsets + num_blocks) % num_blocks
    glob_blocks = lax.broadcasted_iota(jnp.int32, (num_blocks, GLOB), 1)
    key_lists = jnp.concatenate([near_blocks, glob_blocks, rand_rows.astype(jnp.int32)], axis=1)
    list_width = key_lists.shape[1]
    same_block = key_lists[:, :, None] == key_lists[:, None, :]
    lower_slot = lax.broadcasted_iota(jnp.int32, (list_width, list_width), 0) > lax.broadcasted_iota(jnp.int32, (list_width, list_width), 1)
    first_seen = jnp.logical_not(jnp.any(jnp.logical_and(same_block, lower_slot[None]), axis=2))
    return (key_lists, first_seen)

def allowed_tokens(rand_rows, num_blocks):
    key_lists, first_seen = pattern_lists(rand_rows, num_blocks)
    block_ids = lax.broadcasted_iota(jnp.int32, (num_blocks, key_lists.shape[1], num_blocks), 2)
    block_hits = jnp.any(key_lists[:, :, None] == block_ids, axis=1)
    query_ids = lax.broadcasted_iota(jnp.int32, (num_blocks, num_blocks), 0)
    allowed_keys = jnp.logical_or(block_hits, query_ids < GLOB)
    return jnp.repeat(jnp.repeat(allowed_keys, BLOCK, axis=0), BLOCK, axis=1)

def masked_probs(queries, keys_in, allowed_keys, scaling):
    raw_scores = jnp.dot(queries, keys_in.T, preferred_element_type=jnp.float32) * scaling
    raw_scores = jnp.where(allowed_keys, raw_scores, -jnp.inf)
    row_top = lax.optimization_barrier(jnp.max(raw_scores, axis=-1, keepdims=True))
    row_exp = jnp.exp(raw_scores - row_top)
    return row_exp / lax.optimization_barrier(jnp.sum(row_exp, axis=-1, keepdims=True))

def forward_head(queries, keys_in, vals_in, rand_rows):
    scaling = 1.0 / math.sqrt(queries.shape[-1])
    allowed_keys = allowed_tokens(rand_rows, queries.shape[0] // BLOCK)
    weights_low = masked_probs(queries, keys_in, allowed_keys, scaling).astype(jnp.bfloat16)
    return jnp.dot(weights_low, vals_in, preferred_element_type=jnp.float32).astype(jnp.bfloat16)

def backward_head(queries, keys_in, vals_in, grad_mix, rand_rows):
    scaling = 1.0 / math.sqrt(queries.shape[-1])
    allowed_keys = allowed_tokens(rand_rows, queries.shape[0] // BLOCK)
    attn_probs = masked_probs(queries, keys_in, allowed_keys, scaling)
    weights_low = attn_probs.astype(jnp.bfloat16)
    head_out = jnp.dot(weights_low, vals_in, preferred_element_type=jnp.float32).astype(jnp.bfloat16)
    row_delta = lax.optimization_barrier(jnp.sum(grad_mix.astype(jnp.float32) * head_out.astype(jnp.float32), axis=-1, keepdims=True))
    grad_probs = jnp.dot(grad_mix, vals_in.T, preferred_element_type=jnp.float32)
    grad_scores = (attn_probs * (grad_probs - row_delta)).astype(jnp.bfloat16)
    grad_q = (jnp.dot(grad_scores, keys_in, preferred_element_type=jnp.float32) * scaling).astype(jnp.bfloat16)
    grad_k = (jnp.dot(grad_scores.T, queries, preferred_element_type=jnp.float32) * scaling).astype(jnp.bfloat16)
    grad_v = jnp.dot(weights_low.T, grad_mix, preferred_element_type=jnp.float32).astype(jnp.bfloat16)
    return (grad_q, grad_k, grad_v)

def reference(fwd_input, grad_out, w_qkv, w_out, saved_qkv, rand_blocks):
    forward_list = []
    backward_list = []
    for section_index in range(SECTIONS):
        inputs_now = fwd_input[section_index].astype(jnp.float32)
        grads_now = grad_out[section_index].astype(jnp.float32)
        proj_in = w_qkv[section_index].astype(jnp.float32)
        proj_out = w_out[section_index].astype(jnp.float32)
        acts_total = jnp.zeros((3, H, SEQ, DH), jnp.float32)
        mix_total = jnp.zeros((H, SEQ, DH), jnp.float32)
        for group in range(N_TP):
            first = group * DT
            acts_total = acts_total + rounded(jnp.einsum('ld,cdhe->chle', inputs_now[:, first:first + DT], proj_in[:, first:first + DT]))
            mix_total = mix_total + rounded(jnp.einsum('ld,hed->hle', grads_now[:, first:first + DT], proj_out[:, :, first:first + DT]))
        head_acts = acts_total.astype(jnp.bfloat16)
        grad_mixed = mix_total.astype(jnp.bfloat16)
        mixed_heads = lax.map(lambda pack_in: forward_head(pack_in[0], pack_in[1], pack_in[2], pack_in[3]), (head_acts[0], head_acts[1], head_acts[2], rand_blocks[section_index]))
        mixed_wide = mixed_heads.astype(jnp.float32)
        stored = jnp.transpose(saved_qkv[section_index], (0, 2, 1, 3))
        head_grads = lax.map(lambda pack_in: backward_head(pack_in[0], pack_in[1], pack_in[2], pack_in[3], pack_in[4]), (stored[0], stored[1], stored[2], grad_mixed, rand_blocks[section_index]))
        stacked = jnp.stack(head_grads, axis=0).astype(jnp.float32)
        projected = jnp.zeros((SEQ, D), jnp.float32)
        returned = jnp.zeros((SEQ, D), jnp.float32)
        for group in range(N_CTX):
            first = group * HC
            projected = projected + rounded(jnp.einsum('hle,hed->ld', mixed_wide[first:first + HC], proj_out[first:first + HC]))
            returned = returned + rounded(jnp.einsum('chle,cdhe->ld', stacked[:, first:first + HC], proj_in[:, :, first:first + HC]))
        forward_list.append((inputs_now + projected).astype(jnp.bfloat16))
        backward_list.append((grads_now + returned).astype(jnp.bfloat16))
    fwd_next = jnp.roll(jnp.stack(forward_list), 1, axis=0)
    grad_prev = jnp.roll(jnp.stack(backward_list), -1, axis=0)
    return (fwd_next, grad_prev)
```

```python
import math

import jax
import jax.numpy as jnp
from jax import lax
from jax.experimental import pallas as pl
from jax.experimental.pallas import tpu as pltpu
from jax.sharding import PartitionSpec as P

MESH = pl.DeviceIdType.MESH
F32, BF16 = jnp.float32, jnp.bfloat16
T, TB, W, HD = 1024, 128, 1536, 128
PLACES = ((0, 0), (0, 1), (-1, 0), (1, 0), (-1, 1), (1, 1), (2, 0), (2, 1))
N_SEMS = 144


def nn(a, b):
    return lax.dot_general(a, b, (((1,), (0,)), ((), ())), preferred_element_type=F32)


def nt(a, b):
    return lax.dot_general(a, b, (((1,), (1,)), ((), ())), preferred_element_type=F32)


def tn(a, b):
    return lax.dot_general(a, b, (((0,), (0,)), ((), ())), preferred_element_type=F32)


def kernel(fin, gout, wq, wo_in, sv_in, rnd, fnext, gprev, x_b, x_f, w_raw, wp, wo, sv, bias, probs, head_out,
           yp_b, yp_f, y2u_b, y2u_f, y2d_b, y2d_f, ya_b, ya_f, yb_b, yb_f, act_b, act_f, dk, dv, mixed, grads,
           xs_b, xs_f, rz_b, rz_f, rl_b, rl_f, rr_b, rr_f, out_b, out_f, load_sem, send_sem, recv_sem):
    sec, ctx, tp = lax.axis_index("section"), lax.axis_index("ctx"), lax.axis_index("tp")
    zl, xc = ctx // 4, ctx % 4

    def at_place(dx, dz):
        return (zl + dz) % 2 * 4 + (xc + dx + 4) % 4

    owner = [at_place(*place) for place in PLACES]
    right, left, across = {"ctx": owner[3]}, {"ctx": owner[2]}, {"ctx": owner[1]}
    up, down = {"tp": (tp + 1) % 4}, {"tp": (tp + 3) % 4}
    after, before = {"section": (sec + 1) % 8}, {"section": (sec + 7) % 8}
    scale = 1.0 / math.sqrt(HD)

    loads = []

    def load(src, dst):
        copy = pltpu.make_async_copy(src, dst, load_sem.at[len(loads)])
        loads.append(copy)
        copy.start()
        return copy

    sv_loads = [
        load(sv_in.at[:, pl.ds(pl.multiple_of(owner[s] * TB, TB), TB), :], sv.at[:, pl.ds(s * TB, TB), :])
        for s in range(8)
    ]
    own_loads = [load(gout, x_b.at[pl.ds(0, TB)]), load(fin, x_f.at[pl.ds(0, TB)])]
    wo_loads = [
        load(wo_in.at[pl.ds(pl.multiple_of((tp + j) % 4 * HD, HD), HD), :], wo.at[pl.ds(j * HD, HD), :])
        for j in range(4)
    ]
    wq_load = load(wq, w_raw)

    barrier = pltpu.get_barrier_semaphore()
    for other in (right, left, across, up, down, after, before):
        pl.semaphore_signal(barrier, inc=1, device_id=other, device_id_type=MESH)
    pl.semaphore_wait(barrier, 7)

    sent = []

    def msg(src, dst, other):
        k = len(sent)
        copy = pltpu.make_async_remote_copy(
            src_ref=src, dst_ref=dst, send_sem=send_sem.at[k], recv_sem=recv_sem.at[k],
            device_id=other, device_id_type=MESH,
        )
        sent.append(copy)
        return copy

    def part(ref, s, lo=0, hi=TB):
        return ref.at[pl.ds(s * TB + lo, hi - lo)]

    class Flow:
        pass

    flows = []
    for own, x, yp, y2u, y2d, ya, yb, act, heads, xs, rz, rl, rr, out, dest, hop, w in (
        (gout, x_b, yp_b, y2u_b, y2d_b, ya_b, yb_b, act_b, grads, xs_b, rz_b, rl_b, rr_b, out_b, gprev, before, 128),
        (fin, x_f, yp_f, y2u_f, y2d_f, ya_f, yb_f, act_f, mixed, xs_f, rz_f, rl_f, rr_f, out_f, fnext, after, 384),
    ):
        f = Flow()
        f.x, f.yp, f.y2u, f.y2d, f.ya, f.yb, f.act, f.heads = x, yp, y2u, y2d, ya, yb, act, heads
        f.xs, f.out, f.w = xs, out, w
        f.own_r, f.own_l, f.own_z = msg(own, part(x, 2), right), msg(own, part(x, 3), left), msg(own, part(x, 1), across)
        f.fwd_r = msg(part(x, 2, 0, 96), part(x, 6, 0, 96), right)
        f.fwd_l = msg(part(x, 3, 96, 128), part(x, 6, 96, 128), left)
        f.fwd_z2 = msg(part(x, 2, 64, 128), part(x, 4, 64, 128), across)
        f.fwd_z3 = msg(part(x, 3, 64, 128), part(x, 5, 64, 128), across)
        f.z_r = msg(part(x, 1, 0, 64), part(x, 4, 0, 64), right)
        f.z_l = msg(part(x, 1, 0, 64), part(x, 5, 0, 64), left)
        f.z_l2 = msg(part(x, 5, 0, 64), part(x, 7, 0, 64), left)
        f.far_a = msg(part(x, 6, 64, 96), part(x, 7, 64, 96), across)
        f.far_b = msg(part(x, 6, 96, 128), part(x, 7, 96, 128), across)
        f.s2u, f.s2d, f.s1u, f.s1d, f.hu, f.hd, f.h2u, f.h2d = [], [], [], [], [], [], [], []
        v = 512 - w
        f.v = v
        for g in range(4):
            all_rows = pl.ds(g * 256, 256)
            first, last = pl.ds(g * 256, 128), pl.ds(g * 256 + 128, 128)
            f.s2u.append(msg(yp.at[first, pl.ds(2 * w, w)], y2u.at[pl.ds(g * 128, 128)], up))
            f.s2d.append(msg(yp.at[last, pl.ds(2 * w, w)], y2d.at[pl.ds(g * 128, 128)], down))
            f.s1u.append(msg(yp.at[all_rows, pl.ds(w, w)], ya.at[all_rows], up))
            f.s1d.append(msg(yp.at[all_rows, pl.ds(3 * w, w)], yb.at[all_rows], down))
            f.hu.append(msg(heads.at[all_rows, pl.ds(0, v)], heads.at[all_rows, pl.ds(3 * v, v)], up))
            f.hd.append(msg(heads.at[all_rows, pl.ds(0, v)], heads.at[all_rows, pl.ds(v, v)], down))
            f.h2u.append(msg(heads.at[first, pl.ds(3 * v, v)], heads.at[first, pl.ds(2 * v, v)], up))
            f.h2d.append(msg(heads.at[last, pl.ds(v, v)], heads.at[last, pl.ds(2 * v, v)], down))
        f.zb6, f.zb2, f.zb3, f.z0 = (rz.at[pl.ds(a, n)] for a, n in ((0, 64), (64, 64), (128, 64), (192, 128)))
        f.la5, f.la1, f.l3, f.l0 = (rl.at[pl.ds(a, n)] for a, n in ((0, 64), (64, 64), (128, 32), (160, 128)))
        f.ra1, f.r2, f.r0 = (rr.at[pl.ds(a, n)] for a, n in ((0, 64), (64, 96), (160, 128)))
        f.t7r, f.t7z = msg(part(xs, 7, 0, 64), f.la5, right), msg(part(xs, 7, 64, 128), f.zb6, across)
        f.t6l, f.t6r = msg(part(xs, 6, 0, 96), f.r2, left), msg(part(xs, 6, 96, 128), f.l3, right)
        f.t5r, f.t5z = msg(part(xs, 5, 0, 64), f.la1, right), msg(part(xs, 5, 64, 128), f.zb3, across)
        f.t4l, f.t4z = msg(part(xs, 4, 0, 64), f.ra1, left), msg(part(xs, 4, 64, 128), f.zb2, across)
        f.t3r, f.t2l, f.t1z = msg(part(xs, 3), f.l0, right), msg(part(xs, 2), f.r0, left), msg(part(xs, 1), f.z0, across)
        f.hop = msg(out, dest, hop)
        flows.append(f)
    fb, ff = flows

    def start(*copies):
        for copy in copies:
            copy.start()

    def got(*copies):
        for copy in copies:
            copy.wait_recv()

    def send_own(f):
        start(f.own_r, f.own_l, f.own_z)

    def forward_near(f):
        got(f.own_r, f.own_l, f.own_z)
        start(f.fwd_r, f.z_l, f.fwd_z2, f.z_r, f.fwd_z3, f.fwd_l)

    def forward_far(f):
        got(f.z_l)
        start(f.z_l2)
        got(f.fwd_l)
        start(f.far_b)
        got(f.fwd_r)
        start(f.far_a)

    def add_into(dst, lo, n, srcs, cols=None):
        @pl.loop(0, n // 16)
        def _(i):
            r = pl.ds(lo + pl.multiple_of(i * 16, 16), 16)
            c = slice(None) if cols is None else cols
            total = dst[r, c].astype(F32)
            for src in srcs:
                total = total + src[pl.ds(pl.multiple_of(i * 16, 16), 16), :].astype(F32)
            dst[r, c] = total.astype(BF16)

    def project(f, g):
        r = pl.ds(g * 256, 256)

        @pl.loop(0, 4 * f.w // 256)
        def _(n):
            c = pl.ds(pl.multiple_of(n * 256, 256), 256)
            p = nn(f.x[r, :], wp[:, c]) if f is ff else nt(f.x[r, :], wo[c, :])
            f.yp[r, c] = p.astype(BF16)

        start(f.s2u[g], f.s2d[g])

    def sum_two(f, g):
        got(f.s2u[g])
        add_into(f.yp, g * 256, 128, [f.y2u.at[pl.ds(g * 128, 128)]], pl.ds(f.w, f.w))
        start(f.s1u[g])
        got(f.s2d[g])
        add_into(f.yp, g * 256 + 128, 128, [f.y2d.at[pl.ds(g * 128, 128)]], pl.ds(3 * f.w, f.w))
        start(f.s1d[g])

    def sum_all(f, g):
        got(f.s1u[g], f.s1d[g])

        @pl.loop(0, 16)
        def _(i):
            r = pl.ds(g * 256 + pl.multiple_of(i * 16, 16), 16)
            total = f.yp[r, pl.ds(0, f.w)].astype(F32) + f.ya[r, :].astype(F32) + f.yb[r, :].astype(F32)
            f.act[r, :] = total.astype(BF16)

    def make_bias():
        lane = lax.broadcasted_iota(jnp.int32, (8, T), 1)
        key = lane // 64 % 2
        for s in range(8):
            key = key + jnp.where(lane // TB == s, 2 * owner[s], 0)
        for s in range(8):
            for half in range(2):
                q = 2 * owner[s] + half
                ok = (key < 2) | (key == q) | (key == (q + 1) % 16) | (key == (q + 15) % 16)
                for n in range(3):
                    ok = ok | (key == rnd[q, n])
                ok = ok | (jnp.full((8, T), q, jnp.int32) < 2)
                bias[2 * s + half] = jnp.where(ok, 0.0, -1e30).astype(F32)

    def softmax(q, k, b0):
        n = q.shape[0] // 64
        s = nt(q, k).reshape(n, 8, 8, T) * scale + bias[pl.ds(b0, n)].reshape(n, 1, 8, T)
        s = s.reshape(n * 64, T)
        e = jnp.exp(s - jnp.max(s, axis=-1, keepdims=True))
        return (e * (1.0 / jnp.sum(e, axis=-1, keepdims=True))).astype(BF16)

    def saved_probs():
        @pl.loop(0, 8)
        def _(i):
            r = pl.ds(pl.multiple_of(i * 128, 128), 128)
            p = softmax(sv[0, r, :], sv[1], i * 2)
            probs[r, :] = p
            head_out[r, :] = nn(p, sv[2]).astype(BF16)

    def backward_head():
        dk[...] = jnp.zeros_like(dk)
        dv[...] = jnp.zeros_like(dv)

        @pl.loop(0, 4)
        def _(i):
            r = pl.ds(pl.multiple_of(i * 256, 256), 256)
            g = act_b[r, :]
            delta = jnp.sum(g.astype(F32) * head_out[r, :].astype(F32), axis=-1, keepdims=True)
            p = probs[r, :]
            ds = (p.astype(F32) * (nt(g, sv[2]) - delta)).astype(BF16)
            grads[r, pl.ds(0, HD)] = (nn(ds, sv[1]) * scale).astype(BF16)
            dk[...] += tn(ds, sv[0, r, :])
            dv[...] += tn(p, g)

        grads[:, pl.ds(HD, HD)] = (dk[...] * scale).astype(BF16)
        grads[:, pl.ds(2 * HD, HD)] = dv[...].astype(BF16)

    def forward_head(g):
        @pl.loop(0, 2)
        def _(i):
            r = pl.ds(g * 256 + pl.multiple_of(i * 128, 128), 128)
            p = softmax(act_f[r, pl.ds(0, HD)], act_f[:, pl.ds(HD, HD)], g * 4 + i * 2)
            mixed[r, pl.ds(0, HD)] = nn(p, act_f[:, pl.ds(2 * HD, HD)]).astype(BF16)

    def heads_out(f, g):
        start(f.hu[g], f.hd[g])

    def heads_on(f, g):
        got(f.hu[g])
        start(f.h2u[g])
        got(f.hd[g])
        start(f.h2d[g])

    def order_weights():
        row, col = lax.broadcasted_iota(jnp.int32, (256, 256), 0), lax.broadcasted_iota(jnp.int32, (256, 256), 1)
        pick = jnp.where(col == row % 64 * 4 + (row // 64 + tp) % 4, 1.0, 0.0).astype(BF16)
        for c in range(3):
            @pl.loop(0, 12)
            def _(i):
                a = w_raw[pl.ds(pl.multiple_of((c * 24 + i * 2) * 256, 256), 256), :]
                b = w_raw[pl.ds(pl.multiple_of((c * 24 + i * 2 + 1) * 256, 256), 256), :]
                o = nn(pick, jnp.concatenate([a, b], axis=1)).astype(BF16)
                for j in range(4):
                    for k in range(2):
                        wp[pl.ds(pl.multiple_of(i * 128, 128) + k * 64, 64), pl.ds(j * 384 + c * HD, HD)] = (
                            o[j * 64:j * 64 + 64, k * HD:k * HD + HD]
                        )

    def project_back(f, g):
        got(f.h2u[g], f.h2d[g])
        r = pl.ds(g * 256, 256)

        @pl.loop(0, 6)
        def _(n):
            c = pl.ds(pl.multiple_of(n * 256, 256), 256)
            p = nn(f.heads[r, :], wo[:, c]) if f is ff else nt(f.heads[r, :], wp[c, :])
            f.xs[r, c] = p.astype(BF16)

    def back_3(f):
        project_back(f, 3)
        start(f.t7z, f.t7r)

    def back_2(f):
        project_back(f, 2)
        start(f.t4l, f.t5z, f.t4z)
        got(f.t7z)
        add_into(f.xs, 6 * TB + 64, 64, [f.zb6])
        start(f.t6l, f.t6r)
        got(f.t7r)
        add_into(f.xs, 5 * TB, 64, [f.la5])
        start(f.t5r)

    def back_1(f):
        project_back(f, 1)
        got(f.t5z, f.t6r)
        add_into(f.xs, 3 * TB + 64, 64, [f.zb3])
        add_into(f.xs, 3 * TB + 96, 32, [f.l3])
        start(f.t3r)
        got(f.t4z, f.t6l)
        add_into(f.xs, 2 * TB + 64, 64, [f.zb2])
        add_into(f.xs, 2 * TB, 96, [f.r2])
        start(f.t2l)

    def back_0(f):
        project_back(f, 0)
        got(f.t5r, f.t4l)
        add_into(f.xs, TB, 64, [f.la1, f.ra1])
        start(f.t1z)

    def finish(f):
        got(f.t3r, f.t2l, f.t1z)

        @pl.loop(0, 8)
        def _(i):
            r = pl.ds(pl.multiple_of(i * 16, 16), 16)
            total = f.xs[r, :].astype(F32) + f.x[r, :].astype(F32)
            for src in (f.l0, f.r0, f.z0):
                total = total + src[r, :].astype(F32)
            f.out[r, :] = total.astype(BF16)

        start(f.hop)

    send_own(fb)
    make_bias()
    for copy in sv_loads:
        copy.wait()
    saved_probs()
    for copy in own_loads + wo_loads:
        copy.wait()
    forward_near(fb)
    project(fb, 0)
    forward_far(fb)
    send_own(ff)
    project(fb, 1)
    sum_two(fb, 0)
    wq_load.wait()
    order_weights()
    got(fb.z_r, fb.fwd_z2, fb.fwd_z3)
    project(fb, 2)
    sum_two(fb, 1)
    sum_all(fb, 0)
    got(fb.z_l2, fb.far_a, fb.far_b)
    project(fb, 3)
    sum_two(fb, 2)
    sum_all(fb, 1)
    forward_near(ff)
    sum_two(fb, 3)
    sum_all(fb, 2)
    project(ff, 0)
    sum_all(fb, 3)
    backward_head()
    for g in (3, 2, 1, 0):
        heads_out(fb, g)
    forward_far(ff)
    project(ff, 1)
    sum_two(ff, 0)
    heads_on(fb, 3)
    got(ff.z_r, ff.fwd_z2, ff.fwd_z3)
    project(ff, 2)
    sum_two(ff, 1)
    heads_on(fb, 2)
    got(ff.z_l2, ff.far_a, ff.far_b)
    project(ff, 3)
    sum_two(ff, 2)
    sum_all(ff, 0)
    heads_on(fb, 1)
    back_3(fb)
    sum_two(ff, 3)
    sum_all(ff, 1)
    heads_on(fb, 0)
    back_2(fb)
    sum_all(ff, 2)
    sum_all(ff, 3)
    for g in (3, 2, 1, 0):
        forward_head(g)
        heads_out(ff, g)
    back_1(fb)
    heads_on(ff, 3)
    heads_on(ff, 2)
    back_0(fb)
    heads_on(ff, 1)
    heads_on(ff, 0)
    back_3(ff)
    back_2(ff)
    finish(fb)
    back_1(ff)
    back_0(ff)
    finish(ff)
    got(fb.hop, ff.hop)
    for copy in sent:
        copy.wait_send()
    assert len(sent) <= N_SEMS


def per_device(fwd_input, grad_out, w_qkv, w_out, saved_qkv, rand_blocks):
    def vmem(*shape, dtype=BF16):
        return pltpu.VMEM(shape, dtype)

    def pair(rows, width_b, width_f):
        return [vmem(rows, width_b), vmem(rows, width_f)]

    any_space = pl.BlockSpec(memory_space=pl.ANY)
    fwd_next, grad_prev = pl.pallas_call(
        kernel,
        out_shape=[jax.ShapeDtypeStruct((TB, W), BF16)] * 2,
        in_specs=[any_space] * 5 + [pl.BlockSpec(memory_space=pltpu.SMEM)],
        out_specs=[any_space] * 2,
        scratch_shapes=[
            *pair(T, W, W), vmem(12 * W, HD), vmem(W, W), vmem(512, W), vmem(3, T, HD),
            vmem(16, 8, T, dtype=F32), vmem(T, T), vmem(T, HD),
            *pair(T, 512, 1536), *pair(512, 128, 384), *pair(512, 128, 384), *pair(T, 128, 384), *pair(T, 128, 384),
            *pair(T, 128, 384), vmem(T, HD, dtype=F32), vmem(T, HD, dtype=F32), vmem(T, 512), vmem(T, 1536),
            *pair(T, W, W), *pair(320, W, W), *pair(288, W, W), *pair(288, W, W), *pair(TB, W, W),
            pltpu.SemaphoreType.DMA((16,)), pltpu.SemaphoreType.DMA((N_SEMS,)), pltpu.SemaphoreType.DMA((N_SEMS,)),
        ],
        compiler_params=pltpu.CompilerParams(
            collective_id=0, has_side_effects=True, vmem_limit_bytes=62 * 1024 * 1024
        ),
        cost_estimate=pl.CostEstimate(flops=16_000_000_000, bytes_accessed=10_000_000, transcendentals=2_000_000),
    )(
        fwd_input.reshape(TB, W),
        grad_out.reshape(TB, W),
        w_qkv.reshape(12 * W, HD),
        w_out.reshape(512, W),
        saved_qkv.reshape(3, T, HD),
        rand_blocks.reshape(16, 3),
    )
    return (fwd_next[None], grad_prev[None])


def solution(mesh):
    placed = (
        P("section", "ctx", "tp"),
        P("section", "ctx", "tp"),
        P("section", None, "tp", "ctx", None),
        P("section", "ctx", None, "tp"),
        P("section", None, None, ("ctx", "tp"), None),
        P("section", ("ctx", "tp"), None, None),
    )
    return jax.shard_map(
        per_device,
        mesh=mesh,
        in_specs=placed,
        out_specs=(P("section", "ctx", "tp"), P("section", "ctx", "tp")),
        check_vma=False,
    )
```

```python
import math

import jax
import jax.numpy as jnp
from jax import lax
from jax.experimental import pallas as pl
from jax.experimental.pallas import tpu as pltpu
from jax.sharding import PartitionSpec as P

MESH = pl.DeviceIdType.MESH
F32, BF16 = jnp.float32, jnp.bfloat16
T, TB, W, HD = 1024, 128, 1536, 128
PLACES = ((0, 0), (0, 1), (-1, 0), (1, 0), (-1, 1), (1, 1), (2, 0), (2, 1))
GROUPS = ((0, 1), (1, 1), (2, 2), (4, 2), (6, 2))
CUT, MID = 64, 96
LOW = TB - CUT
N_SEMS = 160


def nn(a, b):
    return lax.dot_general(a, b, (((1,), (0,)), ((), ())), preferred_element_type=F32)


def nt(a, b):
    return lax.dot_general(a, b, (((1,), (1,)), ((), ())), preferred_element_type=F32)


def tn(a, b):
    return lax.dot_general(a, b, (((0,), (0,)), ((), ())), preferred_element_type=F32)


def kernel(fin, gout, wq, wo_in, sv_in, rnd, fnext, gprev, x_b, x_f, w_raw, wp, wo, sv, bias, probs, head_out,
           yp_b, yp_f, y2u_b, y2u_f, y2d_b, y2d_f, ya_b, ya_f, yb_b, yb_f, act_b, act_f, dk, dv, mixed, grads,
           xs_b, xs_f, rz_b, rz_f, rl_b, rl_f, rr_b, rr_f, out_b, out_f, load_sem, send_sem, recv_sem):
    sec, ctx, tp = lax.axis_index("section"), lax.axis_index("ctx"), lax.axis_index("tp")
    zl, xc = ctx // 4, ctx % 4

    def at_place(dx, dz):
        return (zl + dz) % 2 * 4 + (xc + dx + 4) % 4

    owner = [at_place(*place) for place in PLACES]
    right, left, across = {"ctx": owner[3]}, {"ctx": owner[2]}, {"ctx": owner[1]}
    up, down = {"tp": (tp + 1) % 4}, {"tp": (tp + 3) % 4}
    sections = lax.axis_size("section")
    after, before = {"section": (sec + 1) % sections}, {"section": (sec + sections - 1) % sections}
    scale = 1.0 / math.sqrt(HD)

    loads = []

    def load(src, dst):
        copy = pltpu.make_async_copy(src, dst, load_sem.at[len(loads)])
        loads.append(copy)
        copy.start()
        return copy

    sv_loads = [
        load(sv_in.at[:, pl.ds(pl.multiple_of(owner[s] * TB, TB), TB), :], sv.at[:, pl.ds(s * TB, TB), :])
        for s in range(8)
    ]
    own_loads = [load(gout, x_b.at[pl.ds(0, TB)]), load(fin, x_f.at[pl.ds(0, TB)])]
    wo_loads = [
        load(wo_in.at[pl.ds(pl.multiple_of((tp + j) % 4 * HD, HD), HD), :], wo.at[pl.ds(j * HD, HD), :])
        for j in range(4)
    ]
    wq_load = load(wq, w_raw)

    barrier = pltpu.get_barrier_semaphore()
    for other in (right, left, across, up, down, after, before):
        pl.semaphore_signal(barrier, inc=1, device_id=other, device_id_type=MESH)
    pl.semaphore_wait(barrier, 7)

    sent = []

    def msg(src, dst, other):
        k = len(sent)
        copy = pltpu.make_async_remote_copy(
            src_ref=src, dst_ref=dst, send_sem=send_sem.at[k], recv_sem=recv_sem.at[k],
            device_id=other, device_id_type=MESH,
        )
        sent.append(copy)
        return copy

    def part(ref, s, lo=0, hi=TB):
        return ref.at[pl.ds(s * TB + lo, hi - lo)]

    class Flow:
        pass

    flows = []
    for own, x, yp, y2u, y2d, ya, yb, act, heads, xs, rz, rl, rr, out, dest, hop, w in (
        (gout, x_b, yp_b, y2u_b, y2d_b, ya_b, yb_b, act_b, grads, xs_b, rz_b, rl_b, rr_b, out_b, gprev, before, 128),
        (fin, x_f, yp_f, y2u_f, y2d_f, ya_f, yb_f, act_f, mixed, xs_f, rz_f, rl_f, rr_f, out_f, fnext, after, 384),
    ):
        f = Flow()
        f.x, f.yp, f.y2u, f.y2d, f.ya, f.yb, f.act, f.heads = x, yp, y2u, y2d, ya, yb, act, heads
        f.xs, f.out, f.w = xs, out, w
        own_part = {0: own.at[pl.ds(0, CUT)], CUT: own.at[pl.ds(CUT, LOW)]}

        def both(s, other):
            return [msg(own_part[lo], part(x, s, lo, hi), other) for lo, hi in ((0, CUT), (CUT, TB))]

        f.own_r, f.own_l, f.own_z = both(2, right), both(3, left), both(1, across)
        f.fwd_r = msg(part(x, 2, 0, CUT), part(x, 6, 0, CUT), right)
        f.fwd_rq = msg(part(x, 2, CUT, MID), part(x, 6, CUT, MID), right)
        f.fwd_l = msg(part(x, 3, MID, TB), part(x, 6, MID, TB), left)
        f.fwd_z2 = msg(part(x, 2, CUT, TB), part(x, 4, CUT, TB), across)
        f.fwd_z3 = msg(part(x, 3, CUT, TB), part(x, 5, CUT, TB), across)
        f.z_r = msg(part(x, 1, 0, CUT), part(x, 4, 0, CUT), right)
        f.z_l = msg(part(x, 1, 0, CUT), part(x, 5, 0, CUT), left)
        f.z_l2 = msg(part(x, 5, 0, CUT), part(x, 7, 0, CUT), left)
        f.far_a = msg(part(x, 6, CUT, MID), part(x, 7, CUT, MID), across)
        f.far_b = msg(part(x, 6, MID, TB), part(x, 7, MID, TB), across)
        f.s2u, f.s2d, f.s1u, f.s1d, f.hu, f.hd, f.h2u, f.h2d = [], [], [], [], [], [], [], []
        v = 512 - w
        f.v = v
        for at, n in GROUPS:
            all_rows, half = pl.ds(at * TB, n * TB), pl.ds(at * TB // 2, n * TB // 2)
            first, last = pl.ds(at * TB, n * TB // 2), pl.ds(at * TB + n * TB // 2, n * TB // 2)
            f.s2u.append(msg(yp.at[first, pl.ds(2 * w, w)], y2u.at[half], up))
            f.s2d.append(msg(yp.at[last, pl.ds(2 * w, w)], y2d.at[half], down))
            f.s1u.append(msg(yp.at[all_rows, pl.ds(w, w)], ya.at[all_rows], up))
            f.s1d.append(msg(yp.at[all_rows, pl.ds(3 * w, w)], yb.at[all_rows], down))
            f.hu.append(msg(heads.at[all_rows, pl.ds(0, v)], heads.at[all_rows, pl.ds(3 * v, v)], up))
            f.hd.append(msg(heads.at[all_rows, pl.ds(0, v)], heads.at[all_rows, pl.ds(v, v)], down))
            f.h2u.append(msg(heads.at[first, pl.ds(3 * v, v)], heads.at[first, pl.ds(2 * v, v)], up))
            f.h2d.append(msg(heads.at[last, pl.ds(v, v)], heads.at[last, pl.ds(2 * v, v)], down))
        def cuts(ref, *sizes):
            at = [sum(sizes[:i]) for i in range(len(sizes))]
            return [ref.at[pl.ds(lo, n)] for lo, n in zip(at, sizes)]

        f.zb6, f.zb2, f.zb3, f.z0a, f.z0b = cuts(rz, LOW, LOW, LOW, CUT, LOW)
        f.la5, f.la1, f.l3, f.l0a, f.l0b = cuts(rl, CUT, CUT, TB - MID, CUT, LOW)
        f.ra1, f.r2a, f.r2q, f.r0a, f.r0b = cuts(rr, CUT, CUT, MID - CUT, CUT, LOW)
        f.t7r, f.t7z = msg(part(xs, 7, 0, CUT), f.la5, right), msg(part(xs, 7, CUT, TB), f.zb6, across)
        f.t6l, f.t6q = msg(part(xs, 6, 0, CUT), f.r2a, left), msg(part(xs, 6, CUT, MID), f.r2q, left)
        f.t6r = msg(part(xs, 6, MID, TB), f.l3, right)
        f.t5r, f.t5z = msg(part(xs, 5, 0, CUT), f.la1, right), msg(part(xs, 5, CUT, TB), f.zb3, across)
        f.t4l, f.t4z = msg(part(xs, 4, 0, CUT), f.ra1, left), msg(part(xs, 4, CUT, TB), f.zb2, across)
        f.t3a, f.t3b = msg(part(xs, 3, 0, CUT), f.l0a, right), msg(part(xs, 3, CUT, TB), f.l0b, right)
        f.t2a, f.t2b = msg(part(xs, 2, 0, CUT), f.r0a, left), msg(part(xs, 2, CUT, TB), f.r0b, left)
        f.t1a, f.t1b = msg(part(xs, 1, 0, CUT), f.z0a, across), msg(part(xs, 1, CUT, TB), f.z0b, across)
        f.hops = [msg(out.at[r], dest.at[r], hop) for r in (pl.ds(0, CUT), pl.ds(CUT, LOW))]
        flows.append(f)
    fb, ff = flows

    def start(*copies):
        for copy in copies:
            copy.start()

    def got(*copies):
        for copy in copies:
            copy.wait_recv()

    def send_own(f):
        start(f.own_z[0], f.own_r[1], f.own_l[1], f.own_z[1], f.own_r[0], f.own_l[0])

    def pass_low(f):
        got(f.own_r[1], f.own_l[1])
        start(f.fwd_z2, f.fwd_z3, f.fwd_rq, f.fwd_l)
        got(f.own_z[0])
        start(f.z_l, f.z_r)

    def pass_high(f):
        got(f.own_r[0])
        start(f.fwd_r)

    def pass_far_low(f):
        got(f.fwd_l)
        start(f.far_b)
        got(f.fwd_rq)
        start(f.far_a)

    def pass_far_high(f):
        got(f.z_l)
        start(f.z_l2)

    def near_here(f):
        got(f.own_z[1], f.own_l[0])

    def diagonal_here(f):
        got(f.z_r, f.fwd_z2, f.fwd_z3)

    def far_here(f):
        got(f.fwd_r, f.z_l2, f.far_a, f.far_b)

    def add_into(dst, lo, n, srcs, cols=None):
        @pl.loop(0, n // 16)
        def _(i):
            r = pl.ds(lo + pl.multiple_of(i * 16, 16), 16)
            c = slice(None) if cols is None else cols
            total = dst[r, c].astype(F32)
            for src in srcs:
                total = total + src[pl.ds(pl.multiple_of(i * 16, 16), 16), :].astype(F32)
            dst[r, c] = total.astype(BF16)

    def rows_of(g):
        return pl.ds(GROUPS[g][0] * TB, GROUPS[g][1] * TB)

    def project(f, g):
        r = rows_of(g)

        @pl.loop(0, 4 * f.w // 256)
        def _(n):
            c = pl.ds(pl.multiple_of(n * 256, 256), 256)
            p = nn(f.x[r, :], wp[:, c]) if f is ff else nt(f.x[r, :], wo[c, :])
            f.yp[r, c] = p.astype(BF16)

        start(f.s2u[g], f.s2d[g])

    def sum_two(f, g):
        at, n = GROUPS[g][0] * TB, GROUPS[g][1] * TB // 2
        got(f.s2u[g])
        add_into(f.yp, at, n, [f.y2u.at[pl.ds(at // 2, n)]], pl.ds(f.w, f.w))
        start(f.s1u[g])
        got(f.s2d[g])
        add_into(f.yp, at + n, n, [f.y2d.at[pl.ds(at // 2, n)]], pl.ds(3 * f.w, f.w))
        start(f.s1d[g])

    def sum_all(f, g):
        got(f.s1u[g], f.s1d[g])

        @pl.loop(0, GROUPS[g][1] * 8)
        def _(i):
            r = pl.ds(GROUPS[g][0] * TB + pl.multiple_of(i * 16, 16), 16)
            total = f.yp[r, pl.ds(0, f.w)].astype(F32) + f.ya[r, :].astype(F32) + f.yb[r, :].astype(F32)
            f.act[r, :] = total.astype(BF16)

    def make_bias():
        lane = lax.broadcasted_iota(jnp.int32, (8, T), 1)
        key = lane // 64 % 2
        for s in range(8):
            key = key + jnp.where(lane // TB == s, 2 * owner[s], 0)
        for s in range(8):
            for half in range(2):
                q = 2 * owner[s] + half
                ok = (key < 2) | (key == q) | (key == (q + 1) % 16) | (key == (q + 15) % 16)
                for n in range(3):
                    ok = ok | (key == rnd[n, 0, q])
                ok = ok | (jnp.full((8, T), q, jnp.int32) < 2)
                bias[2 * s + half] = jnp.where(ok, 0.0, -1e30).astype(F32)

    def softmax(q, k, b0):
        n = q.shape[0] // 64
        s = nt(q, k).reshape(n, 8, 8, T) * scale + bias[pl.ds(b0, n)].reshape(n, 1, 8, T)
        s = s.reshape(n * 64, T)
        e = jnp.exp(s - jnp.max(s, axis=-1, keepdims=True))
        return (e * (1.0 / jnp.sum(e, axis=-1, keepdims=True))).astype(BF16)

    def saved_probs(quarter):
        @pl.loop(quarter * 2, quarter * 2 + 2)
        def _(i):
            r = pl.ds(pl.multiple_of(i * 128, 128), 128)
            p = softmax(sv[0, r, :], sv[1], i * 2)
            probs[r, :] = p
            head_out[r, :] = nn(p, sv[2]).astype(BF16)

    def backward_head():
        dk[...] = jnp.zeros_like(dk)
        dv[...] = jnp.zeros_like(dv)

        @pl.loop(0, 4)
        def _(i):
            r = pl.ds(pl.multiple_of(i * 256, 256), 256)
            g = act_b[r, :]
            delta = jnp.sum(g.astype(F32) * head_out[r, :].astype(F32), axis=-1, keepdims=True)
            p = probs[r, :]
            ds = (p.astype(F32) * (nt(g, sv[2]) - delta)).astype(BF16)
            grads[r, pl.ds(0, HD)] = (nn(ds, sv[1]) * scale).astype(BF16)
            dk[...] += tn(ds, sv[0, r, :])
            dv[...] += tn(p, g)

        grads[:, pl.ds(HD, HD)] = (dk[...] * scale).astype(BF16)
        grads[:, pl.ds(2 * HD, HD)] = dv[...].astype(BF16)

    def forward_head(g):
        @pl.loop(0, GROUPS[g][1])
        def _(i):
            r = pl.ds(GROUPS[g][0] * TB + pl.multiple_of(i * TB, TB), TB)
            p = softmax(act_f[r, pl.ds(0, HD)], act_f[:, pl.ds(HD, HD)], (GROUPS[g][0] + i) * 2)
            mixed[r, pl.ds(0, HD)] = nn(p, act_f[:, pl.ds(2 * HD, HD)]).astype(BF16)

    def heads_out(f, g):
        start(f.hu[g], f.hd[g])

    def heads_on(f, g):
        got(f.hu[g])
        start(f.h2u[g])
        got(f.hd[g])
        start(f.h2d[g])

    def order_weights():
        row, col = lax.broadcasted_iota(jnp.int32, (256, 256), 0), lax.broadcasted_iota(jnp.int32, (256, 256), 1)
        pick = jnp.where(col == row % 64 * 4 + (row // 64 + tp) % 4, 1.0, 0.0).astype(BF16)
        for c in range(3):
            @pl.loop(0, 12, unroll=4)
            def _(i):
                a = w_raw[pl.ds(pl.multiple_of((c * 24 + i * 2) * 256, 256), 256), :]
                b = w_raw[pl.ds(pl.multiple_of((c * 24 + i * 2 + 1) * 256, 256), 256), :]
                o = nn(pick, jnp.concatenate([a, b], axis=1)).astype(BF16)
                for j in range(4):
                    for k in range(2):
                        wp[pl.ds(pl.multiple_of(i * 128, 128) + k * 64, 64), pl.ds(j * 384 + c * HD, HD)] = (
                            o[j * 64:j * 64 + 64, k * HD:k * HD + HD]
                        )

    def project_back(f, g):
        got(f.h2u[g], f.h2d[g])
        r = rows_of(g)

        @pl.loop(0, 6)
        def _(n):
            c = pl.ds(pl.multiple_of(n * 256, 256), 256)
            p = nn(f.heads[r, :], wo[:, c]) if f is ff else nt(f.heads[r, :], wp[c, :])
            f.xs[r, c] = p.astype(BF16)

    def back_4(f):
        project_back(f, 4)
        start(f.t7z, f.t7r, f.t6l)

    def add_4z(f):
        got(f.t7z)
        add_into(f.xs, 6 * TB + CUT, LOW, [f.zb6])
        start(f.t6q, f.t6r)

    def back_3(f):
        project_back(f, 3)
        start(f.t5z, f.t4z, f.t4l)

    def add_3x(f):
        got(f.t7r)
        add_into(f.xs, 5 * TB, CUT, [f.la5])
        start(f.t5r)

    def back_2(f):
        project_back(f, 2)
        start(f.t3a)

    def add_2x(f):
        got(f.t6l)
        add_into(f.xs, 2 * TB, CUT, [f.r2a])
        start(f.t2a)

    def add_2z(f):
        got(f.t5z, f.t6r)
        add_into(f.xs, 3 * TB + CUT, LOW, [f.zb3])
        add_into(f.xs, 3 * TB + MID, TB - MID, [f.l3])
        start(f.t3b)
        got(f.t4z, f.t6q)
        add_into(f.xs, 2 * TB + CUT, LOW, [f.zb2])
        add_into(f.xs, 2 * TB + CUT, MID - CUT, [f.r2q])
        start(f.t2b)

    def back_1(f):
        project_back(f, 1)
        start(f.t1b)

    def add_1x(f):
        got(f.t5r, f.t4l)
        add_into(f.xs, TB, CUT, [f.la1, f.ra1])
        start(f.t1a)

    def finish(f, lo, n, srcs, hop):
        @pl.loop(0, n // 16)
        def _(i):
            at = pl.multiple_of(i * 16, 16)
            r = pl.ds(lo + at, 16)
            total = f.xs[r, :].astype(F32) + f.x[r, :].astype(F32)
            for src in srcs:
                total = total + src[pl.ds(at, 16), :].astype(F32)
            f.out[r, :] = total.astype(BF16)

        start(hop)

    def finish_high(f):
        got(f.t3a, f.t2a, f.t1a)
        finish(f, 0, CUT, (f.l0a, f.r0a, f.z0a), f.hops[0])

    def finish_low(f):
        got(f.t3b, f.t2b, f.t1b)
        finish(f, CUT, LOW, (f.l0b, f.r0b, f.z0b), f.hops[1])

    send_own(ff)
    make_bias()
    wq_load.wait()
    order_weights()
    for copy in own_loads + wo_loads:
        copy.wait()
    project(ff, 0)
    pass_low(ff)
    for copy in sv_loads:
        copy.wait()
    saved_probs(0)
    sum_two(ff, 0)
    saved_probs(1)
    pass_high(ff)
    near_here(ff)
    project(ff, 1)
    pass_far_low(ff)
    project(ff, 2)
    pass_far_high(ff)
    send_own(fb)
    sum_all(ff, 0)
    sum_two(ff, 1)
    diagonal_here(ff)
    project(ff, 3)
    sum_two(ff, 2)
    sum_all(ff, 1)
    far_here(ff)
    project(ff, 4)
    sum_two(ff, 3)
    saved_probs(2)
    sum_all(ff, 2)
    pass_low(fb)
    sum_two(ff, 4)
    saved_probs(3)
    project(fb, 0)
    pass_high(fb)
    near_here(fb)
    project(fb, 1)
    project(fb, 2)
    sum_all(ff, 3)
    pass_far_low(fb)
    sum_two(fb, 0)
    sum_two(fb, 1)
    pass_far_high(fb)
    sum_all(ff, 4)
    forward_head(4)
    heads_out(ff, 4)
    sum_two(fb, 2)
    forward_head(3)
    heads_out(ff, 3)
    diagonal_here(fb)
    project(fb, 3)
    heads_on(ff, 4)
    forward_head(2)
    heads_out(ff, 2)
    heads_on(ff, 3)
    far_here(fb)
    project(fb, 4)
    sum_two(fb, 3)
    back_4(ff)
    forward_head(1)
    heads_out(ff, 1)
    forward_head(0)
    heads_out(ff, 0)
    heads_on(ff, 2)
    sum_two(fb, 4)
    sum_all(fb, 0)
    sum_all(fb, 1)
    sum_all(fb, 2)
    back_3(ff)
    add_4z(ff)
    heads_on(ff, 1)
    heads_on(ff, 0)
    sum_all(fb, 3)
    sum_all(fb, 4)
    backward_head()
    heads_out(fb, 4)
    heads_out(fb, 3)
    add_3x(ff)
    back_2(ff)
    add_2x(ff)
    back_1(ff)
    heads_on(fb, 4)
    heads_out(fb, 2)
    add_1x(ff)
    add_2z(ff)
    project_back(ff, 0)
    heads_on(fb, 3)
    heads_out(fb, 1)
    heads_out(fb, 0)
    back_4(fb)
    finish_high(ff)
    finish_low(ff)
    heads_on(fb, 2)
    add_4z(fb)
    back_3(fb)
    add_3x(fb)
    heads_on(fb, 1)
    heads_on(fb, 0)
    back_2(fb)
    add_2x(fb)
    back_1(fb)
    add_1x(fb)
    add_2z(fb)
    project_back(fb, 0)
    finish_high(fb)
    finish_low(fb)
    got(*fb.hops, *ff.hops)
    for copy in sent:
        copy.wait_send()
    assert len(sent) <= N_SEMS


def hand_over(a, b, a_out, b_out):
    a_out[...] = a[...]
    b_out[...] = b[...]


def per_device(fwd_input, grad_out, w_qkv, w_out, saved_qkv, rand_blocks):
    def vmem(*shape, dtype=BF16):
        return pltpu.VMEM(shape, dtype)

    def pair(rows, width_b, width_f):
        return [vmem(rows, width_b), vmem(rows, width_f)]

    any_space = pl.BlockSpec(memory_space=pl.ANY)
    fwd_next, grad_prev = pl.pallas_call(
        kernel,
        out_shape=[jax.ShapeDtypeStruct((TB, W), BF16)] * 2,
        in_specs=[any_space] * 5 + [pl.BlockSpec(memory_space=pltpu.SMEM)],
        out_specs=[any_space] * 2,
        scratch_shapes=[
            *pair(T, W, W), vmem(12 * W, HD), vmem(W, W), vmem(512, W), vmem(3, T, HD),
            vmem(16, 8, T, dtype=F32), vmem(T, T), vmem(T, HD),
            *pair(T, 512, 1536), *pair(512, 128, 384), *pair(512, 128, 384), *pair(T, 128, 384), *pair(T, 128, 384),
            *pair(T, 128, 384), vmem(T, HD, dtype=F32), vmem(T, HD, dtype=F32), vmem(T, 512), vmem(T, 1536),
            *pair(T, W, W), *pair(TB + 3 * LOW, W, W), *pair(TB + 2 * CUT + TB - MID, W, W), *pair(TB + CUT + MID, W, W), *pair(TB, W, W),
            pltpu.SemaphoreType.DMA((16,)), pltpu.SemaphoreType.DMA((N_SEMS,)), pltpu.SemaphoreType.DMA((N_SEMS,)),
        ],
        compiler_params=pltpu.CompilerParams(
            collective_id=0, has_side_effects=True, vmem_limit_bytes=62 * 1024 * 1024
        ),
        cost_estimate=pl.CostEstimate(flops=16_000_000_000, bytes_accessed=10_000_000, transcendentals=2_000_000),
    )(
        fwd_input.reshape(TB, W),
        grad_out.reshape(TB, W),
        w_qkv.reshape(12 * W, HD),
        w_out.reshape(512, W),
        saved_qkv.reshape(3, T, HD),
        rand_blocks.transpose(0, 3, 1, 2).reshape(3, 1, 16),
    )
    block = pl.BlockSpec((TB // 2, W), lambda i: (i, 0))
    fwd_next, grad_prev = pl.pallas_call(
        hand_over,
        grid=(2,),
        out_shape=[jax.ShapeDtypeStruct((TB, W), BF16)] * 2,
        in_specs=[block] * 2,
        out_specs=[block] * 2,
    )(fwd_next, grad_prev)
    return (fwd_next[None], grad_prev[None])


def solution(mesh):
    placed = (
        P("section", "ctx", "tp"),
        P("section", "ctx", "tp"),
        P("section", None, "tp", "ctx", None),
        P("section", "ctx", None, "tp"),
        P("section", None, None, ("ctx", "tp"), None),
        P("section", ("ctx", "tp"), None, None),
    )
    return jax.shard_map(
        per_device,
        mesh=mesh,
        in_specs=placed,
        out_specs=(P("section", "ctx", "tp"), P("section", "ctx", "tp")),
        check_vma=False,
    )
```

```python
import math

import jax
import jax.numpy as jnp
from jax import lax
from jax.experimental import pallas as pl
from jax.experimental.pallas import tpu as pltpu
from jax.sharding import PartitionSpec as P

MESH = pl.DeviceIdType.MESH
F32, BF16 = jnp.float32, jnp.bfloat16
T, TB, W, HD = 1024, 128, 1536, 128
PLACES = ((0, 0), (0, 1), (-1, 0), (1, 0), (-1, 1), (1, 1), (2, 0), (2, 1))
ORDER = (
    (0, 0), (0, 1), (2, 1), (3, 1), (1, 0), (2, 0), (3, 0), (1, 1),
    (6, 1), (4, 1), (4, 0), (5, 0), (5, 1), (6, 0), (7, 0), (7, 1),
)
ROW = {block: 64 * i for i, block in enumerate(ORDER)}
GROUPS = (
    ((0, 2), (2, 3), (5, 3), (8, 4), (12, 4)),
    ((0, 2), (2, 3), (5, 3), (8, 2), (10, 2), (12, 2), (14, 2)),
)
RESULTS = ((0, 2), (2, 2), (4, 3), (7, 1), (8, 4), (12, 2), (14, 2))
CUT, MID = 64, 96
LOW = TB - CUT
N_SENT, N_SEMS = 64, 190


def nn(a, b):
    return lax.dot_general(a, b, (((1,), (0,)), ((), ())), preferred_element_type=F32)


def nt(a, b):
    return lax.dot_general(a, b, (((1,), (1,)), ((), ())), preferred_element_type=F32)


def tn(a, b):
    return lax.dot_general(a, b, (((0,), (0,)), ((), ())), preferred_element_type=F32)


def kernel(fin, gout, wq, wo_in, sv_in, rnd, fnext, gprev, x_b, x_f, w_raw, wp, wo, sv, bias, probs, head_out,
           yp_b, yp_f, y2u_b, y2u_f, y2d_b, y2d_f, ya_b, ya_f, yb_b, yb_f, act_b, act_f, dk, dv, mixed, grads,
           xs_b, xs_f, rz_b, rz_f, rl_b, rl_f, rr_b, rr_f, out_b, out_f, load_sem, send_sem, recv_sem):
    sec, ctx, tp = lax.axis_index("section"), lax.axis_index("ctx"), lax.axis_index("tp")
    zl, xc = ctx // 4, ctx % 4

    def at_place(dx, dz):
        return (zl + dz) % 2 * 4 + (xc + dx + 4) % 4

    owner = [at_place(*place) for place in PLACES]
    right, left, across = {"ctx": owner[3]}, {"ctx": owner[2]}, {"ctx": owner[1]}
    up, down = {"tp": (tp + 1) % 4}, {"tp": (tp + 3) % 4}
    sections = lax.axis_size("section")
    after, before = {"section": (sec + 1) % sections}, {"section": (sec + sections - 1) % sections}
    scale = 1.0 / math.sqrt(HD)

    loads = []

    def load(src, dst):
        copy = pltpu.make_async_copy(src, dst, load_sem.at[len(loads)])
        loads.append(copy)
        copy.start()
        return copy

    sv_loads = [
        load(
            sv_in.at[:, pl.ds(pl.multiple_of(owner[s] * TB + half * 64, 64), 64), :],
            sv.at[:, pl.ds(ROW[s, half], 64), :],
        )
        for s, half in ORDER
    ]
    own_loads = [load(gout, x_b.at[pl.ds(0, TB)]), load(fin, x_f.at[pl.ds(0, TB)])]
    wo_loads = [
        load(wo_in.at[pl.ds(pl.multiple_of((tp + j) % 4 * HD, HD), HD), :], wo.at[pl.ds(j * HD, HD), :])
        for j in range(4)
    ]
    wq_load = load(wq, w_raw)

    barrier = pltpu.get_barrier_semaphore()
    for other in (right, left, across, up, down, after, before):
        pl.semaphore_signal(barrier, inc=1, device_id=other, device_id_type=MESH)
    pl.semaphore_wait(barrier, 7)

    count, pending, free = [0], [], list(range(N_SENT))

    class Message:
        def __init__(self, src, dst, other):
            self.ends = (src, dst, other)
            self.k = count[0]
            count[0] += 1

        def copy(self, slot):
            src, dst, other = self.ends
            return pltpu.make_async_remote_copy(
                src_ref=src, dst_ref=dst, send_sem=send_sem.at[slot], recv_sem=recv_sem.at[self.k],
                device_id=other, device_id_type=MESH,
            )

    def msg(src, dst, other):
        return Message(src, dst, other)

    def row(s, lo):
        return ROW[s, lo // CUT] + lo % CUT

    def part(ref, s, lo, hi):
        return ref.at[pl.ds(row(s, lo), hi - lo)]

    class Flow:
        pass

    flows = []
    for own, x, yp, y2u, y2d, ya, yb, act, heads, xs, rz, rl, rr, out, dest, hop, w in (
        (gout, x_b, yp_b, y2u_b, y2d_b, ya_b, yb_b, act_b, grads, xs_b, rz_b, rl_b, rr_b, out_b, gprev, before, 128),
        (fin, x_f, yp_f, y2u_f, y2d_f, ya_f, yb_f, act_f, mixed, xs_f, rz_f, rl_f, rr_f, out_f, fnext, after, 384),
    ):
        f = Flow()
        f.x, f.yp, f.y2u, f.y2d, f.ya, f.yb, f.act, f.heads = x, yp, y2u, y2d, ya, yb, act, heads
        f.xs, f.out, f.w = xs, out, w
        own_part = {0: own.at[pl.ds(0, CUT)], CUT: own.at[pl.ds(CUT, LOW)]}

        def both(s, other):
            return [msg(own_part[lo], part(x, s, lo, hi), other) for lo, hi in ((0, CUT), (CUT, TB))]

        f.own_r, f.own_l, f.own_z = both(2, right), both(3, left), both(1, across)
        f.fwd_r = msg(part(x, 2, 0, CUT), part(x, 6, 0, CUT), right)
        f.fwd_rq = msg(part(x, 2, CUT, MID), part(x, 6, CUT, MID), right)
        f.fwd_l = msg(part(x, 3, MID, TB), part(x, 6, MID, TB), left)
        f.fwd_z2 = msg(part(x, 2, CUT, TB), part(x, 4, CUT, TB), across)
        f.fwd_z3 = msg(part(x, 3, CUT, TB), part(x, 5, CUT, TB), across)
        f.z_r = msg(part(x, 1, 0, CUT), part(x, 4, 0, CUT), right)
        f.z_l = msg(part(x, 1, 0, CUT), part(x, 5, 0, CUT), left)
        f.z_l2 = msg(part(x, 5, 0, CUT), part(x, 7, 0, CUT), left)
        f.far_a = msg(part(x, 6, CUT, MID), part(x, 7, CUT, MID), across)
        f.far_b = msg(part(x, 6, MID, TB), part(x, 7, MID, TB), across)
        f.s2u, f.s2d, f.s1u, f.s1d = [], [], [], []
        f.groups = GROUPS[w == 384]
        for at, n in f.groups:
            all_rows, half = pl.ds(at * 64, n * 64), pl.ds(at * 32, n * 32)
            first, last = pl.ds(at * 64, n * 32), pl.ds(at * 64 + n * 32, n * 32)
            f.s2u.append(msg(yp.at[first, pl.ds(2 * w, w)], y2u.at[half], up))
            f.s2d.append(msg(yp.at[last, pl.ds(2 * w, w)], y2d.at[half], down))
            f.s1u.append(msg(yp.at[all_rows, pl.ds(w, w)], ya.at[all_rows], up))
            f.s1d.append(msg(yp.at[all_rows, pl.ds(3 * w, w)], yb.at[all_rows], down))

        def round_y(groups, at_col, v):
            hu, hd, h2u, h2d = [], [], [], []
            for at, n in groups:
                all_rows = pl.ds(at * 64, n * 64)
                first, last = pl.ds(at * 64, n * 32), pl.ds(at * 64 + n * 32, n * 32)
                c = [pl.ds(heads.shape[1] // 4 * j + at_col, v) for j in range(4)]
                hu.append(msg(heads.at[all_rows, c[0]], heads.at[all_rows, c[3]], up))
                hd.append(msg(heads.at[all_rows, c[0]], heads.at[all_rows, c[1]], down))
                h2u.append(msg(heads.at[first, c[3]], heads.at[first, c[2]], up))
                h2d.append(msg(heads.at[last, c[1]], heads.at[last, c[2]], down))
            return hu, hd, h2u, h2d

        if w == 384:
            f.results = round_y(RESULTS, 0, HD)
        else:
            f.results = round_y(RESULTS, HD, 2 * HD)
            f.queries = round_y(f.groups, 0, HD)
        def cuts(ref, *sizes):
            at = [sum(sizes[:i]) for i in range(len(sizes))]
            return [ref.at[pl.ds(lo, n)] for lo, n in zip(at, sizes)]

        f.zb6, f.zb2, f.zb3, f.z0a, f.z0b = cuts(rz, LOW, LOW, LOW, CUT, LOW)
        f.la5, f.la1, f.l3, f.l0a, f.l0b = cuts(rl, CUT, CUT, TB - MID, CUT, LOW)
        f.ra1, f.r2a, f.r2q, f.r0a, f.r0b = cuts(rr, CUT, CUT, MID - CUT, CUT, LOW)
        f.t7r, f.t7z = msg(part(xs, 7, 0, CUT), f.la5, right), msg(part(xs, 7, CUT, TB), f.zb6, across)
        f.t6l, f.t6q = msg(part(xs, 6, 0, CUT), f.r2a, left), msg(part(xs, 6, CUT, MID), f.r2q, left)
        f.t6r = msg(part(xs, 6, MID, TB), f.l3, right)
        f.t5r, f.t5z = msg(part(xs, 5, 0, CUT), f.la1, right), msg(part(xs, 5, CUT, TB), f.zb3, across)
        f.t4l, f.t4z = msg(part(xs, 4, 0, CUT), f.ra1, left), msg(part(xs, 4, CUT, TB), f.zb2, across)
        f.t3a, f.t3b = msg(part(xs, 3, 0, CUT), f.l0a, right), msg(part(xs, 3, CUT, TB), f.l0b, right)
        f.t2a, f.t2b = msg(part(xs, 2, 0, CUT), f.r0a, left), msg(part(xs, 2, CUT, TB), f.r0b, left)
        f.t1a, f.t1b = msg(part(xs, 1, 0, CUT), f.z0a, across), msg(part(xs, 1, CUT, TB), f.z0b, across)
        f.hops = [msg(out.at[r], dest.at[r], hop) for r in (pl.ds(0, CUT), pl.ds(CUT, LOW))]
        flows.append(f)
    fb, ff = flows

    def drain(n):
        for copy, slot in pending[:n]:
            copy.wait_send()
            free.append(slot)
        del pending[:n]

    def start(*messages):
        for message in messages:
            if not free:
                drain(8)
            slot = free.pop(0)
            copy = message.copy(slot)
            copy.start()
            pending.append((copy, slot))

    def got(*messages):
        for message in messages:
            message.copy(0).wait_recv()

    def send_own(f):
        start(f.own_z[0], f.own_r[1], f.own_l[1], f.own_z[1], f.own_r[0], f.own_l[0])

    def pass_low(f):
        got(f.own_r[1], f.own_l[1])
        start(f.fwd_z2, f.fwd_z3, f.fwd_rq, f.fwd_l)
        got(f.own_z[0])
        start(f.z_l, f.z_r)

    def pass_high(f):
        got(f.own_r[0])
        start(f.fwd_r)

    def pass_far_low(f):
        got(f.fwd_l)
        start(f.far_b)
        got(f.fwd_rq)
        start(f.far_a)

    def pass_far_high(f):
        got(f.z_l)
        start(f.z_l2)

    def near_here(f):
        got(f.own_z[1], f.own_l[0])

    def diagonal_here(f):
        got(f.z_r, f.fwd_z2)

    def far_here(f):
        got(f.fwd_z3, f.fwd_r, f.z_l2, f.far_a, f.far_b)

    def add_into(dst, lo, n, srcs, cols=None):
        @pl.loop(0, n // 16)
        def _(i):
            r = pl.ds(lo + pl.multiple_of(i * 16, 16), 16)
            c = slice(None) if cols is None else cols
            total = dst[r, c].astype(F32)
            for src in srcs:
                total = total + src[pl.ds(pl.multiple_of(i * 16, 16), 16), :].astype(F32)
            dst[r, c] = total.astype(BF16)

    def rows_of(f, g):
        return pl.ds(f.groups[g][0] * 64, f.groups[g][1] * 64)

    def project(f, g):
        r = rows_of(f, g)

        @pl.loop(0, 4 * f.w // 256, unroll=min(3, 4 * f.w // 256))
        def _(n):
            c = pl.ds(pl.multiple_of(n * 256, 256), 256)
            p = nn(f.x[r, :], wp[:, c]) if f is ff else nt(f.x[r, :], wo[c, :])
            f.yp[r, c] = p.astype(BF16)

        start(f.s2u[g], f.s2d[g])

    def sum_two(f, g):
        at, n = f.groups[g][0] * 64, f.groups[g][1] * 32
        got(f.s2u[g])
        add_into(f.yp, at, n, [f.y2u.at[pl.ds(at // 2, n)]], pl.ds(f.w, f.w))
        start(f.s1u[g])
        got(f.s2d[g])
        add_into(f.yp, at + n, n, [f.y2d.at[pl.ds(at // 2, n)]], pl.ds(3 * f.w, f.w))
        start(f.s1d[g])

    def sum_all(f, g):
        got(f.s1u[g], f.s1d[g])

        @pl.loop(0, f.groups[g][1] * 4)
        def _(i):
            r = pl.ds(f.groups[g][0] * 64 + pl.multiple_of(i * 16, 16), 16)
            total = f.yp[r, pl.ds(0, f.w)].astype(F32) + f.ya[r, :].astype(F32) + f.yb[r, :].astype(F32)
            f.act[r, :] = total.astype(BF16)

    def make_bias():
        lane = lax.broadcasted_iota(jnp.int32, (8, T), 1)
        lane_block = lane // 64
        key = jnp.zeros((8, T), jnp.int32)
        for i, (s, half) in enumerate(ORDER):
            key = jnp.where(lane_block == i, 2 * owner[s] + half, key)
        for i, (s, half) in enumerate(ORDER):
            q = 2 * owner[s] + half
            ok = (key < 2) | (key == q) | (key == (q + 1) % 16) | (key == (q + 15) % 16)
            for n in range(3):
                ok = ok | (key == rnd[n, 0, q])
            ok = ok | (jnp.full((8, T), q, jnp.int32) < 2)
            bias[i] = jnp.where(ok, 0.0, -1e30).astype(F32)

    def softmax(q, k, b0):
        n = q.shape[0] // 64
        s = nt(q, k).reshape(n, 8, 8, T) * scale + bias[pl.ds(b0, n)].reshape(n, 1, 8, T)
        s = s.reshape(n * 64, T)
        e = jnp.exp(s - jnp.max(s, axis=-1, keepdims=True))
        return (e * (1.0 / jnp.sum(e, axis=-1, keepdims=True))).astype(BF16)

    def saved_probs(quarter):
        @pl.loop(quarter * 2, quarter * 2 + 2)
        def _(i):
            r = pl.ds(pl.multiple_of(i * 128, 128), 128)
            p = softmax(sv[0, r, :], sv[1], i * 2)
            probs[r, :] = p
            head_out[r, :] = nn(p, sv[2]).astype(BF16)

    def backward_start():
        dk[...] = jnp.zeros_like(dk)
        dv[...] = jnp.zeros_like(dv)

    def backward_rows(g):
        r = rows_of(fb, g)
        grad = act_b[r, :]
        delta = jnp.sum(grad.astype(F32) * head_out[r, :].astype(F32), axis=-1, keepdims=True)
        p = probs[r, :]
        ds = (p.astype(F32) * (nt(grad, sv[2]) - delta)).astype(BF16)
        grads[r, pl.ds(0, HD)] = (nn(ds, sv[1]) * scale).astype(BF16)
        start(fb.queries[0][g], fb.queries[1][g])
        dk[...] += tn(ds, sv[0, r, :])
        dv[...] += tn(p, grad)

    def queries_on(g):
        got(fb.queries[0][g])
        start(fb.queries[2][g])
        got(fb.queries[1][g])
        start(fb.queries[3][g])

    def queries_here(*groups):
        for g in groups:
            got(fb.queries[2][g], fb.queries[3][g])

    def backward_end():
        grads[:, pl.ds(HD, HD)] = (dk[...] * scale).astype(BF16)
        grads[:, pl.ds(2 * HD, HD)] = dv[...].astype(BF16)

    def forward_head(g):
        at, n = RESULTS[g]
        size = 128 if n % 2 == 0 else n * 64

        @pl.loop(0, n * 64 // size)
        def _(i):
            r = pl.ds(at * 64 + pl.multiple_of(i * size, 64), size)
            p = softmax(act_f[r, pl.ds(0, HD)], act_f[:, pl.ds(HD, HD)], at + i * (size // 64))
            mixed[r, pl.ds(0, HD)] = nn(p, act_f[:, pl.ds(2 * HD, HD)]).astype(BF16)

        start(ff.results[0][g], ff.results[1][g])

    def heads_out(f, g):
        start(f.results[0][g], f.results[1][g])

    def heads_on(f, g):
        got(f.results[0][g])
        start(f.results[2][g])
        got(f.results[1][g])
        start(f.results[3][g])

    def order_weights():
        row, col = lax.broadcasted_iota(jnp.int32, (256, 256), 0), lax.broadcasted_iota(jnp.int32, (256, 256), 1)
        pick = jnp.where(col == row % 64 * 4 + (row // 64 + tp) % 4, 1.0, 0.0).astype(BF16)
        for c in range(3):
            @pl.loop(0, 12, unroll=4)
            def _(i):
                a = w_raw[pl.ds(pl.multiple_of((c * 24 + i * 2) * 256, 256), 256), :]
                b = w_raw[pl.ds(pl.multiple_of((c * 24 + i * 2 + 1) * 256, 256), 256), :]
                o = nn(pick, jnp.concatenate([a, b], axis=1)).astype(BF16)
                for j in range(4):
                    for k in range(2):
                        wp[pl.ds(pl.multiple_of(i * 128, 128) + k * 64, 64), pl.ds(j * 384 + c * HD, HD)] = (
                            o[j * 64:j * 64 + 64, k * HD:k * HD + HD]
                        )

    def project_back(f, g):
        got(f.results[2][g], f.results[3][g])
        r = pl.ds(RESULTS[g][0] * 64, RESULTS[g][1] * 64)

        @pl.loop(0, 6, unroll=3)
        def _(n):
            c = pl.ds(pl.multiple_of(n * 256, 256), 256)
            p = nn(f.heads[r, :], wo[:, c]) if f is ff else nt(f.heads[r, :], wp[c, :])
            f.xs[r, c] = p.astype(BF16)

    def back_6(f):
        project_back(f, 6)
        start(f.t7z, f.t7r)

    def back_5(f):
        project_back(f, 5)
        start(f.t6l, f.t5z)

    def back_4(f):
        project_back(f, 4)
        start(f.t4l, f.t4z)

    def add_6(f):
        got(f.t7z)
        add_into(f.xs, row(6, CUT), LOW, [f.zb6])
        start(f.t6q, f.t6r)

    def add_5(f):
        got(f.t7r)
        add_into(f.xs, row(5, 0), CUT, [f.la5])
        start(f.t5r)

    def back_3(f):
        project_back(f, 3)
        start(f.t1b)

    def back_2(f):
        project_back(f, 2)
        start(f.t3a)
        got(f.t6l)
        add_into(f.xs, row(2, 0), CUT, [f.r2a])
        start(f.t2a)

    def add_1(f):
        got(f.t5r, f.t4l)
        add_into(f.xs, row(1, 0), CUT, [f.la1, f.ra1])
        start(f.t1a)

    def back_1(f):
        project_back(f, 1)
        got(f.t5z, f.t6r)
        add_into(f.xs, row(3, CUT), LOW, [f.zb3])
        add_into(f.xs, row(3, MID), TB - MID, [f.l3])
        start(f.t3b)
        got(f.t4z, f.t6q)
        add_into(f.xs, row(2, CUT), LOW, [f.zb2])
        add_into(f.xs, row(2, CUT), MID - CUT, [f.r2q])
        start(f.t2b)

    def finish(f, lo, n, srcs, hop):
        @pl.loop(0, n // 16)
        def _(i):
            at = pl.multiple_of(i * 16, 16)
            r = pl.ds(lo + at, 16)
            total = f.xs[r, :].astype(F32) + f.x[r, :].astype(F32)
            for src in srcs:
                total = total + src[pl.ds(at, 16), :].astype(F32)
            f.out[r, :] = total.astype(BF16)

        start(hop)

    def finish_high(f):
        got(f.t3a, f.t2a, f.t1a)
        finish(f, 0, CUT, (f.l0a, f.r0a, f.z0a), f.hops[0])

    def finish_low(f):
        got(f.t3b, f.t2b, f.t1b)
        finish(f, CUT, LOW, (f.l0b, f.r0b, f.z0b), f.hops[1])

    send_own(ff)
    make_bias()
    wq_load.wait()
    order_weights()
    for copy in own_loads + wo_loads:
        copy.wait()
    project(ff, 0)
    pass_low(ff)
    project(ff, 1)
    sum_two(ff, 0)
    pass_high(ff)
    near_here(ff)
    project(ff, 2)
    pass_far_low(ff)
    sum_two(ff, 1)
    sum_all(ff, 0)
    for copy in sv_loads:
        copy.wait()
    saved_probs(0)
    pass_far_high(ff)
    send_own(fb)
    sum_two(ff, 2)
    got(ff.fwd_z2)
    project(ff, 3)
    got(ff.z_r)
    project(ff, 4)
    sum_all(ff, 1)
    sum_two(ff, 3)
    got(ff.fwd_z3, ff.fwd_r)
    project(ff, 5)
    sum_two(ff, 4)
    got(ff.z_l2, ff.far_a, ff.far_b)
    project(ff, 6)
    sum_all(ff, 2)
    pass_low(fb)
    sum_two(ff, 5)
    project(fb, 0)
    project(fb, 1)
    sum_two(ff, 6)
    sum_all(ff, 3)
    saved_probs(1)
    pass_high(fb)
    near_here(fb)
    project(fb, 2)
    pass_far_low(fb)
    sum_all(ff, 4)
    sum_two(fb, 0)
    saved_probs(2)
    sum_all(ff, 5)
    sum_two(fb, 1)
    sum_all(ff, 6)
    forward_head(6)
    pass_far_high(fb)
    forward_head(5)
    sum_two(fb, 2)
    forward_head(4)
    heads_on(ff, 6)
    diagonal_here(fb)
    project(fb, 3)
    forward_head(3)
    forward_head(2)
    heads_on(ff, 5)
    sum_two(fb, 3)
    forward_head(1)
    forward_head(0)
    back_6(ff)
    far_here(fb)
    project(fb, 4)
    heads_on(ff, 4)
    sum_all(fb, 0)
    sum_all(fb, 1)
    back_5(ff)
    sum_two(fb, 4)
    saved_probs(3)
    backward_start()
    backward_rows(0)
    backward_rows(1)
    heads_on(ff, 3)
    heads_on(ff, 2)
    sum_all(fb, 2)
    backward_rows(2)
    back_4(ff)
    add_6(ff)
    add_5(ff)
    sum_all(fb, 3)
    backward_rows(3)
    sum_all(fb, 4)
    backward_rows(4)
    backward_end()
    heads_out(fb, 6)
    heads_out(fb, 5)
    heads_on(ff, 1)
    heads_on(ff, 0)
    queries_on(0)
    queries_on(1)
    queries_on(2)
    back_3(ff)
    queries_on(3)
    queries_on(4)
    heads_on(fb, 6)
    heads_out(fb, 4)
    back_2(ff)
    add_1(ff)
    heads_on(fb, 5)
    back_1(ff)
    heads_out(fb, 3)
    heads_out(fb, 2)
    queries_here(4)
    back_6(fb)
    heads_on(fb, 4)
    heads_out(fb, 1)
    heads_out(fb, 0)
    project_back(ff, 0)
    back_5(fb)
    finish_high(ff)
    finish_low(ff)
    queries_here(3)
    back_4(fb)
    add_6(fb)
    add_5(fb)
    heads_on(fb, 3)
    heads_on(fb, 2)
    queries_here(2)
    back_3(fb)
    heads_on(fb, 1)
    heads_on(fb, 0)
    queries_here(1)
    back_2(fb)
    add_1(fb)
    back_1(fb)
    queries_here(0)
    project_back(fb, 0)
    finish_high(fb)
    finish_low(fb)
    got(*fb.hops, *ff.hops)
    drain(len(pending))
    assert count[0] == N_SEMS, count


def hand_over(a, b, a_out, b_out):
    a_out[...] = a[...]
    b_out[...] = b[...]


def per_device(fwd_input, grad_out, w_qkv, w_out, saved_qkv, rand_blocks):
    def vmem(*shape, dtype=BF16):
        return pltpu.VMEM(shape, dtype)

    def pair(rows, width_b, width_f):
        return [vmem(rows, width_b), vmem(rows, width_f)]

    any_space = pl.BlockSpec(memory_space=pl.ANY)
    fwd_next, grad_prev = pl.pallas_call(
        kernel,
        out_shape=[jax.ShapeDtypeStruct((TB, W), BF16)] * 2,
        in_specs=[any_space] * 5 + [pl.BlockSpec(memory_space=pltpu.SMEM)],
        out_specs=[any_space] * 2,
        scratch_shapes=[
            *pair(T, W, W), vmem(12 * W, HD), vmem(W, W), vmem(512, W), vmem(3, T, HD),
            vmem(16, 8, T, dtype=F32), vmem(T, T), vmem(T, HD),
            *pair(T, 512, 1536), *pair(512, 128, 384), *pair(512, 128, 384), *pair(T, 128, 384), *pair(T, 128, 384),
            *pair(T, 128, 384), vmem(T, HD, dtype=F32), vmem(T, HD, dtype=F32), vmem(T, 512), vmem(T, 1536),
            *pair(T, W, W), *pair(TB + 3 * LOW, W, W), *pair(TB + 2 * CUT + TB - MID, W, W), *pair(TB + CUT + MID, W, W), *pair(TB, W, W),
            pltpu.SemaphoreType.DMA((24,)), pltpu.SemaphoreType.DMA((N_SENT,)), pltpu.SemaphoreType.DMA((N_SEMS,)),
        ],
        compiler_params=pltpu.CompilerParams(
            collective_id=0, has_side_effects=True, vmem_limit_bytes=62 * 1024 * 1024
        ),
        cost_estimate=pl.CostEstimate(flops=16_000_000_000, bytes_accessed=10_000_000, transcendentals=2_000_000),
    )(
        fwd_input.reshape(TB, W),
        grad_out.reshape(TB, W),
        w_qkv.reshape(12 * W, HD),
        w_out.reshape(512, W),
        saved_qkv.reshape(3, T, HD),
        rand_blocks.transpose(0, 3, 1, 2).reshape(3, 1, 16),
    )
    block = pl.BlockSpec((TB // 2, W), lambda i: (i, 0))
    fwd_next, grad_prev = pl.pallas_call(
        hand_over,
        grid=(2,),
        out_shape=[jax.ShapeDtypeStruct((TB, W), BF16)] * 2,
        in_specs=[block] * 2,
        out_specs=[block] * 2,
    )(fwd_next, grad_prev)
    return (fwd_next[None], grad_prev[None])


def solution(mesh):
    placed = (
        P("section", "ctx", "tp"),
        P("section", "ctx", "tp"),
        P("section", None, "tp", "ctx", None),
        P("section", "ctx", None, "tp"),
        P("section", None, None, ("ctx", "tp"), None),
        P("section", ("ctx", "tp"), None, None),
    )
    return jax.shard_map(
        per_device,
        mesh=mesh,
        in_specs=placed,
        out_specs=(P("section", "ctx", "tp"), P("section", "ctx", "tp")),
        check_vma=False,
    )
```

```python
import functools
import math
import types

import jax
import jax.numpy as jnp
from jax import lax
from jax.experimental import pallas as pl
from jax.experimental.pallas import tpu as pltpu
from jax.sharding import PartitionSpec as P

MESH = pl.DeviceIdType.MESH
F32, BF16 = jnp.float32, jnp.bfloat16
T, TB, W, HD = 1024, 128, 1536, 128
PLACES = ((0, 0), (0, 1), (-1, 0), (1, 0), (-1, 1), (1, 1), (2, 0), (2, 1))
ORDER = (
    (0, 0), (0, 1), (2, 1), (3, 1), (1, 0), (2, 0), (3, 0), (1, 1),
    (6, 1), (4, 1), (4, 0), (5, 0), (5, 1), (6, 0), (7, 0), (7, 1),
)
ROW = {block: 64 * i for i, block in enumerate(ORDER)}
GROUPS = (
    ((0, 2), (2, 3), (5, 3), (8, 4), (12, 4)),
    ((0, 2), (2, 3), (5, 3), (8, 2), (10, 2), (12, 2), (14, 2)),
)
RESULTS = ((0, 2), (2, 2), (4, 3), (7, 1), (8, 4), (12, 2), (14, 2))
CUT, MID, SIDE = 64, 96, 112
LOW = TB - CUT
N_SENT, N_SEMS = 64, 198


def nn(a, b):
    return lax.dot_general(a, b, (((1,), (0,)), ((), ())), preferred_element_type=F32)


def nt(a, b):
    return lax.dot_general(a, b, (((1,), (1,)), ((), ())), preferred_element_type=F32)


def tn(a, b):
    return lax.dot_general(a, b, (((0,), (0,)), ((), ())), preferred_element_type=F32)


def kernel(fin, gout, wq, wo_in, sv_in, rnd, fnext, gprev, x_b, x_f, w_raw, wp, wo, sv, bias, probs, head_out,
           yp_b, yp_f, y2u_b, y2u_f, y2d_b, y2d_f, ya_b, ya_f, yb_b, yb_f, act_b, act_f, dk, dv, mixed, grads,
           xs_b, xs_f, rz_b, rz_f, rl_b, rl_f, rr_b, rr_f, out_b, out_f, pick, wpt, load_sem, send_sem, recv_sem):
    sec, ctx, tp = lax.axis_index("section"), lax.axis_index("ctx"), lax.axis_index("tp")
    zl, xc = ctx // 4, ctx % 4

    def at_place(dx, dz):
        return (zl + dz) % 2 * 4 + (xc + dx + 4) % 4

    owner = [at_place(*place) for place in PLACES]
    right, left, across = {"ctx": owner[3]}, {"ctx": owner[2]}, {"ctx": owner[1]}
    up, down = {"tp": (tp + 1) % 4}, {"tp": (tp + 3) % 4}
    sections = lax.axis_size("section")
    after, before = {"section": (sec + 1) % sections}, {"section": (sec + sections - 1) % sections}
    scale = 1.0 / math.sqrt(HD)

    loads = []

    def load(src, dst):
        copy = pltpu.make_async_copy(src, dst, load_sem.at[len(loads)])
        loads.append(copy)
        copy.start()
        return copy

    sv_loads = [
        load(
            sv_in.at[:, pl.ds(pl.multiple_of(owner[s] * TB + half * 64, 64), 64), :],
            sv.at[:, pl.ds(ROW[s, half], 64), :],
        )
        for s, half in ORDER
    ]
    own_loads = [load(gout, x_b.at[pl.ds(0, TB)]), load(fin, x_f.at[pl.ds(0, TB)])]
    wo_loads = [
        load(wo_in.at[pl.ds(pl.multiple_of((tp + j) % 4 * HD, HD), HD), :], wo.at[pl.ds(j * HD, HD), :])
        for j in range(4)
    ]
    wq_loads = [load(wq, w_raw)]

    barrier = pltpu.get_barrier_semaphore()
    for other in (right, left, across, up, down, after, before):
        pl.semaphore_signal(barrier, inc=1, device_id=other, device_id_type=MESH)
    pl.semaphore_wait(barrier, 7)

    count, pending, free = [0], [], list(range(N_SENT))

    class Message:
        def __init__(self, src, dst, other):
            self.ends = (src, dst, other)
            self.k = count[0]
            count[0] += 1

        def copy(self, slot):
            src, dst, other = self.ends
            return pltpu.make_async_remote_copy(
                src_ref=src, dst_ref=dst, send_sem=send_sem.at[slot], recv_sem=recv_sem.at[self.k],
                device_id=other, device_id_type=MESH,
            )

    def msg(src, dst, other):
        return Message(src, dst, other)

    def row(s, lo):
        return ROW[s, lo // CUT] + lo % CUT

    def part(ref, s, lo, hi):
        return ref.at[pl.ds(row(s, lo), hi - lo)]

    class Flow:
        pass

    flows = []
    for own, x, yp, y2u, y2d, ya, yb, act, heads, xs, rz, rl, rr, out, dest, hop, w in (
        (gout, x_b, yp_b, y2u_b, y2d_b, ya_b, yb_b, act_b, grads, xs_b, rz_b, rl_b, rr_b, out_b, gprev, before, 128),
        (fin, x_f, yp_f, y2u_f, y2d_f, ya_f, yb_f, act_f, mixed, xs_f, rz_f, rl_f, rr_f, out_f, fnext, after, 384),
    ):
        f = Flow()
        f.x, f.yp, f.y2u, f.y2d, f.ya, f.yb, f.act, f.heads = x, yp, y2u, y2d, ya, yb, act, heads
        f.xs, f.out, f.w = xs, out, w
        own_part = {0: own.at[pl.ds(0, CUT)], CUT: own.at[pl.ds(CUT, LOW)]}

        def both(s, other):
            return [msg(own_part[lo], part(x, s, lo, hi), other) for lo, hi in ((0, CUT), (CUT, TB))]

        f.own_r, f.own_l, f.own_z = both(2, right), both(3, left), both(1, across)
        f.fwd_r = msg(part(x, 2, 0, CUT), part(x, 6, 0, CUT), right)
        f.fwd_rq = msg(part(x, 2, CUT, MID), part(x, 6, CUT, MID), right)
        f.fwd_l = msg(part(x, 3, MID, TB), part(x, 6, MID, TB), left)
        f.fwd_z2 = msg(part(x, 2, CUT, SIDE), part(x, 4, CUT, SIDE), across)
        f.fwd_z3 = msg(part(x, 3, CUT, SIDE), part(x, 5, CUT, SIDE), across)
        f.z_r = msg(part(x, 1, 0, CUT), part(x, 4, 0, CUT), right)
        f.z_l = msg(part(x, 1, 0, CUT), part(x, 5, 0, CUT), left)
        f.z_rq = msg(part(x, 1, SIDE, TB), part(x, 4, SIDE, TB), right)
        f.z_lq = msg(part(x, 1, SIDE, TB), part(x, 5, SIDE, TB), left)
        f.z_l2 = msg(part(x, 5, 0, CUT), part(x, 7, 0, CUT), left)
        f.far_a = msg(part(x, 6, CUT, MID), part(x, 7, CUT, MID), across)
        f.far_b = msg(part(x, 6, MID, TB), part(x, 7, MID, TB), across)
        f.s2u, f.s2d, f.s1u, f.s1d = [], [], [], []
        f.groups = GROUPS[w == 384]
        for at, n in f.groups:
            all_rows, half = pl.ds(at * 64, n * 64), pl.ds(at * 32, n * 32)
            first, last = pl.ds(at * 64, n * 32), pl.ds(at * 64 + n * 32, n * 32)
            f.s2u.append(msg(yp.at[first, pl.ds(2 * w, w)], y2u.at[half], up))
            f.s2d.append(msg(yp.at[last, pl.ds(2 * w, w)], y2d.at[half], down))
            f.s1u.append(msg(yp.at[all_rows, pl.ds(w, w)], ya.at[all_rows], up))
            f.s1d.append(msg(yp.at[all_rows, pl.ds(3 * w, w)], yb.at[all_rows], down))

        def round_y(groups, at_col, v):
            hu, hd, h2u, h2d = [], [], [], []
            for at, n in groups:
                all_rows = pl.ds(at * 64, n * 64)
                first, last = pl.ds(at * 64, n * 32), pl.ds(at * 64 + n * 32, n * 32)
                c = [pl.ds(heads.shape[1] // 4 * j + at_col, v) for j in range(4)]
                hu.append(msg(heads.at[all_rows, c[0]], heads.at[all_rows, c[3]], up))
                hd.append(msg(heads.at[all_rows, c[0]], heads.at[all_rows, c[1]], down))
                h2u.append(msg(heads.at[first, c[3]], heads.at[first, c[2]], up))
                h2d.append(msg(heads.at[last, c[1]], heads.at[last, c[2]], down))
            return hu, hd, h2u, h2d

        if w == 384:
            f.results = round_y(RESULTS, 0, HD)
        else:
            f.results = round_y(RESULTS, HD, 2 * HD)
            f.queries = round_y(f.groups, 0, HD)
        def cuts(ref, *sizes):
            at = [sum(sizes[:i]) for i in range(len(sizes))]
            return [ref.at[pl.ds(lo, n)] for lo, n in zip(at, sizes)]

        f.zb6, f.zb2, f.zb3, f.z0a, f.z0b = cuts(rz, LOW, SIDE - CUT, SIDE - CUT, CUT, LOW)
        f.la5, f.la1, f.l3, f.l0a, f.l0b, f.lb1 = cuts(rl, CUT, CUT, TB - MID, CUT, LOW, TB - SIDE)
        f.ra1, f.r2a, f.r2q, f.r0a, f.r0b, f.rb1 = cuts(rr, CUT, CUT, MID - CUT, CUT, LOW, TB - SIDE)
        f.t7r, f.t7z = msg(part(xs, 7, 0, CUT), f.la5, right), msg(part(xs, 7, CUT, TB), f.zb6, across)
        f.t6l, f.t6q = msg(part(xs, 6, 0, CUT), f.r2a, left), msg(part(xs, 6, CUT, MID), f.r2q, left)
        f.t6r = msg(part(xs, 6, MID, TB), f.l3, right)
        f.t5r, f.t5z = msg(part(xs, 5, 0, CUT), f.la1, right), msg(part(xs, 5, CUT, SIDE), f.zb3, across)
        f.t4l, f.t4z = msg(part(xs, 4, 0, CUT), f.ra1, left), msg(part(xs, 4, CUT, SIDE), f.zb2, across)
        f.t5q, f.t4q = msg(part(xs, 5, SIDE, TB), f.lb1, right), msg(part(xs, 4, SIDE, TB), f.rb1, left)
        f.t3a, f.t3b = msg(part(xs, 3, 0, CUT), f.l0a, right), msg(part(xs, 3, CUT, TB), f.l0b, right)
        f.t2a, f.t2b = msg(part(xs, 2, 0, CUT), f.r0a, left), msg(part(xs, 2, CUT, TB), f.r0b, left)
        f.t1a, f.t1b = msg(part(xs, 1, 0, CUT), f.z0a, across), msg(part(xs, 1, CUT, TB), f.z0b, across)
        f.hops = [msg(out.at[r], dest.at[r], hop) for r in (pl.ds(0, CUT), pl.ds(CUT, LOW))]
        flows.append(f)
    fb, ff = flows

    def drain(n):
        for copy, slot in pending[:n]:
            copy.wait_send()
            free.append(slot)
        del pending[:n]

    def start(*messages):
        for message in messages:
            if not free:
                drain(8)
            slot = free.pop(0)
            copy = message.copy(slot)
            copy.start()
            pending.append((copy, slot))

    seen = set()

    def got(*messages):
        for message in messages:
            if message.k not in seen:
                seen.add(message.k)
                message.copy(0).wait_recv()

    def need(copies):
        while copies:
            copies.pop().wait()

    def here(f, block):
        s, half = block
        return {
            (0, 0): (), (0, 1): (), (1, 0): (f.own_z[0],), (1, 1): (f.own_z[1],), (2, 0): (f.own_r[0],),
            (2, 1): (f.own_r[1],), (3, 0): (f.own_l[0],), (3, 1): (f.own_l[1],), (4, 0): (f.z_r,), (4, 1): (f.fwd_z2, f.z_rq),
            (5, 0): (f.z_l,), (5, 1): (f.fwd_z3, f.z_lq), (6, 0): (f.fwd_r,), (6, 1): (f.fwd_rq, f.fwd_l), (7, 0): (f.z_l2,),
            (7, 1): (f.far_a, f.far_b),
        }[block]

    def pass_on(arrived, *onward):
        def step():
            got(*arrived)
            start(*onward)

        return step

    def add_into(dst, lo, n, srcs, cols=None):
        @pl.loop(0, n // 16)
        def _(i):
            r = pl.ds(lo + pl.multiple_of(i * 16, 16), 16)
            c = slice(None) if cols is None else cols
            total = dst[r, c].astype(F32)
            for src in srcs:
                total = total + src[pl.ds(pl.multiple_of(i * 16, 16), 16), :].astype(F32)
            dst[r, c] = total.astype(BF16)

    def rows_of(f, g):
        return pl.ds(f.groups[g][0] * 64, f.groups[g][1] * 64)

    def project(f, g):
        at, n = f.groups[g]
        for block in ORDER[at:at + n]:
            got(*here(f, block))
        need(own_loads)
        need(wo_loads)
        r = rows_of(f, g)

        @pl.loop(0, 4 * f.w // 256, unroll=min(3, 4 * f.w // 256))
        def _(n):
            c = pl.ds(pl.multiple_of(n * 256, 256), 256)
            p = nn(f.x[r, :], wp[:, c]) if f is ff else nt(f.x[r, :], wo[c, :])
            f.yp[r, c] = p.astype(BF16)

        start(f.s2u[g], f.s2d[g])

    def sum_two(f, g):
        at, n = f.groups[g][0] * 64, f.groups[g][1] * 32
        got(f.s2u[g])
        add_into(f.yp, at, n, [f.y2u.at[pl.ds(at // 2, n)]], pl.ds(f.w, f.w))
        start(f.s1u[g])
        got(f.s2d[g])
        add_into(f.yp, at + n, n, [f.y2d.at[pl.ds(at // 2, n)]], pl.ds(3 * f.w, f.w))
        start(f.s1d[g])

    def sum_all(f, g):
        got(f.s1u[g], f.s1d[g])

        @pl.loop(0, f.groups[g][1] * 4)
        def _(i):
            r = pl.ds(f.groups[g][0] * 64 + pl.multiple_of(i * 16, 16), 16)
            total = f.yp[r, pl.ds(0, f.w)].astype(F32) + f.ya[r, :].astype(F32) + f.yb[r, :].astype(F32)
            f.act[r, :] = total.astype(BF16)

    def make_bias():
        lane = lax.broadcasted_iota(jnp.int32, (8, T), 1)
        lane_block = lane // 64
        key = jnp.zeros((8, T), jnp.int32)
        for i, (s, half) in enumerate(ORDER):
            key = jnp.where(lane_block == i, 2 * owner[s] + half, key)
        for i, (s, half) in enumerate(ORDER):
            q = 2 * owner[s] + half
            ok = (key < 2) | (key == q) | (key == (q + 1) % 16) | (key == (q + 15) % 16)
            for n in range(3):
                ok = ok | (key == rnd[n, 0, q])
            ok = ok | (jnp.full((8, T), q, jnp.int32) < 2)
            bias[i] = jnp.where(ok, 0.0, -1e30).astype(F32)

    def softmax(q, k, b0):
        n = q.shape[0] // 64
        s = nt(q, k).reshape(n, 8, 8, T) * scale + bias[pl.ds(b0, n)].reshape(n, 1, 8, T)
        s = s.reshape(n * 64, T)
        e = jnp.exp(s - jnp.max(s, axis=-1, keepdims=True))
        return (e * (1.0 / jnp.sum(e, axis=-1, keepdims=True))).astype(BF16)

    def saved_probs(quarter):
        need(sv_loads)

        @pl.loop(quarter * 2, quarter * 2 + 2)
        def _(i):
            r = pl.ds(pl.multiple_of(i * 128, 128), 128)
            p = softmax(sv[0, r, :], sv[1], i * 2)
            probs[r, :] = p
            head_out[r, :] = nn(p, sv[2]).astype(BF16)

    begun = []

    def backward_rows(g):
        if not begun:
            begun.append(g)
            dk[...] = jnp.zeros_like(dk)
            dv[...] = jnp.zeros_like(dv)
        r = rows_of(fb, g)
        grad = act_b[r, :]
        delta = jnp.sum(grad.astype(F32) * head_out[r, :].astype(F32), axis=-1, keepdims=True)
        p = probs[r, :]
        ds = (p.astype(F32) * (nt(grad, sv[2]) - delta)).astype(BF16)
        grads[r, pl.ds(0, HD)] = (nn(ds, sv[1]) * scale).astype(BF16)
        start(fb.queries[0][g], fb.queries[1][g])
        dk[...] += tn(ds, sv[0, r, :])
        dv[...] += tn(p, grad)

    def queries_on(g):
        got(fb.queries[0][g])
        start(fb.queries[2][g])
        got(fb.queries[1][g])
        start(fb.queries[3][g])

    def backward_end():
        grads[:, pl.ds(HD, HD)] = (dk[...] * scale).astype(BF16)
        grads[:, pl.ds(2 * HD, HD)] = dv[...].astype(BF16)

    def forward_head(g):
        at, n = RESULTS[g]
        size = 128 if n % 2 == 0 else n * 64

        @pl.loop(0, n * 64 // size)
        def _(i):
            r = pl.ds(at * 64 + pl.multiple_of(i * size, 64), size)
            p = softmax(act_f[r, pl.ds(0, HD)], act_f[:, pl.ds(HD, HD)], at + i * (size // 64))
            mixed[r, pl.ds(0, HD)] = nn(p, act_f[:, pl.ds(2 * HD, HD)]).astype(BF16)

        start(ff.results[0][g], ff.results[1][g])

    def heads_out(f, g):
        start(f.results[0][g], f.results[1][g])

    def heads_on(f, g):
        got(f.results[0][g])
        start(f.results[2][g])
        got(f.results[1][g])
        start(f.results[3][g])

    def order_weights():
        need(wq_loads)
        row, col = lax.broadcasted_iota(jnp.int32, (256, 256), 0), lax.broadcasted_iota(jnp.int32, (256, 256), 1)
        pick = jnp.where(col == row % 64 * 4 + (row // 64 + tp) % 4, 1.0, 0.0).astype(BF16)
        for c in range(3):
            @pl.loop(0, 12, unroll=4)
            def _(i):
                a = w_raw[pl.ds(pl.multiple_of((c * 24 + i * 2) * 256, 256), 256), :]
                b = w_raw[pl.ds(pl.multiple_of((c * 24 + i * 2 + 1) * 256, 256), 256), :]
                o = nn(pick, jnp.concatenate([a, b], axis=1)).astype(BF16)
                for j in range(4):
                    for k in range(2):
                        wp[pl.ds(pl.multiple_of(i * 128, 128) + k * 64, 64), pl.ds(j * 384 + c * HD, HD)] = (
                            o[j * 64:j * 64 + 64, k * HD:k * HD + HD]
                        )

    turned = []

    def turn_weights(c):
        if not turned:
            turned.append(c)
            row_id, col_id = (lax.broadcasted_iota(jnp.int32, (512, 512), k) for k in (0, 1))
            pick[...] = jnp.where(row_id == col_id % 128 * 4 + (col_id // 128 + tp) % 4, 1.0, 0.0).astype(BF16)

        @pl.loop(0, 12, unroll=3)
        def _(i):
            o = tn(w_raw[pl.ds(pl.multiple_of((c * 12 + i) * 512, 512), 512), :], pick[...]).astype(BF16)
            for j in range(4):
                wpt[pl.ds(j * 384 + c * HD, HD), pl.ds(pl.multiple_of(i * 128, 128), 128)] = o[:, j * HD:j * HD + HD]

    def project_back(f, g):
        got(f.results[2][g], f.results[3][g])
        if f is fb:
            at, n = RESULTS[g]
            for k, (first, number) in enumerate(fb.groups):
                if first < at + n and at < first + number:
                    got(fb.queries[2][k], fb.queries[3][k])
        r = pl.ds(RESULTS[g][0] * 64, RESULTS[g][1] * 64)

        @pl.loop(0, 6, unroll=3)
        def _(n):
            c = pl.ds(pl.multiple_of(n * 256, 256), 256)
            p = nn(f.heads[r, :], wo[:, c]) if f is ff else nn(f.heads[r, :], wpt[:, c])
            f.xs[r, c] = p.astype(BF16)

    def back(f, g):
        project_back(f, g)
        start(*{6: (f.t7z, f.t7r), 5: (f.t5z, f.t6l, f.t5q), 4: (f.t4z, f.t4l, f.t4q), 2: (f.t3a,)}.get(g, ()))

    def combine(f, arrived, adds, *onward):
        def step():
            got(*arrived)
            for at, n, srcs in adds:
                add_into(f.xs, at, n, srcs)
            start(*onward)

        return step

    def finish(f, lo, n, srcs, hop):
        @pl.loop(0, n // 16)
        def _(i):
            at = pl.multiple_of(i * 16, 16)
            r = pl.ds(lo + at, 16)
            total = f.xs[r, :].astype(F32) + f.x[r, :].astype(F32)
            for src in srcs:
                total = total + src[pl.ds(at, 16), :].astype(F32)
            f.out[r, :] = total.astype(BF16)

        start(hop)

    def finish_high(f):
        got(f.t3a, f.t2a, f.t1a)
        finish(f, 0, CUT, (f.l0a, f.r0a, f.z0a), f.hops[0])

    def finish_low(f):
        got(f.t3b, f.t2b, f.t1b)
        finish(f, CUT, LOW, (f.l0b, f.r0b, f.z0b), f.hops[1])

    for f in flows:
        f.do = types.SimpleNamespace(
            own1=pass_on((), f.own_z[0], f.own_r[1], f.own_l[1]),
            own2=pass_on((), f.own_z[1], f.own_r[0], f.own_l[0]),
            pz2=pass_on((f.own_r[1],), f.fwd_z2, f.fwd_rq),
            pz3=pass_on((f.own_l[1],), f.fwd_z3, f.fwd_l),
            pzl=pass_on((f.own_z[0],), f.z_l, f.z_r),
            pzs=pass_on((f.own_z[1],), f.z_rq, f.z_lq),
            pr=pass_on((f.own_r[0],), f.fwd_r),
            pfb=pass_on((f.fwd_l,), f.far_b),
            pfa=pass_on((f.fwd_rq,), f.far_a),
            pl2=pass_on((f.z_l,), f.z_l2),
            a6=combine(f, (f.t7z,), ((row(6, CUT), LOW, [f.zb6]),), f.t6q, f.t6r),
            a5=combine(f, (f.t7r,), ((row(5, 0), CUT, [f.la5]),), f.t5r),
            a2=combine(f, (f.t6l,), ((row(2, 0), CUT, [f.r2a]),), f.t2a),
            a1=combine(f, (f.t5r, f.t4l), ((row(1, 0), CUT, [f.la1, f.ra1]),), f.t1a),
            a1b=combine(f, (f.t5q, f.t4q), ((row(1, SIDE), TB - SIDE, [f.lb1, f.rb1]),), f.t1b),
            a3b=combine(
                f, (f.t5z, f.t6r), ((row(3, CUT), SIDE - CUT, [f.zb3]), (row(3, MID), TB - MID, [f.l3])), f.t3b
            ),
            a2b=combine(
                f, (f.t4z, f.t6q), ((row(2, CUT), SIDE - CUT, [f.zb2]), (row(2, CUT), MID - CUT, [f.r2q])), f.t2b
            ),
            finA=lambda f=f: finish_high(f),
            finB=lambda f=f: finish_low(f),
            proj=[functools.partial(project, f, g) for g in range(len(f.groups))],
            two=[functools.partial(sum_two, f, g) for g in range(len(f.groups))],
            total=[functools.partial(sum_all, f, g) for g in range(len(f.groups))],
            on=[functools.partial(heads_on, f, g) for g in range(len(RESULTS))],
            back=[functools.partial(back, f, g) for g in range(len(RESULTS))],
        )
    fwd, bwd = ff.do, fb.do

    fwd.own1()
    fwd.own2()
    order_weights()
    fwd.proj[0]()
    fwd.pzl()
    fwd.pz3()
    fwd.proj[1]()
    bwd.proj[0]()
    fwd.pz2()
    fwd.two[0]()
    fwd.proj[2]()
    fwd.pzs()
    fwd.two[1]()
    fwd.proj[4]()
    fwd.pr()
    make_bias()
    fwd.pl2()
    fwd.pfb()
    fwd.pfa()
    fwd.two[2]()
    bwd.own1()
    saved_probs(2)
    bwd.own2()
    fwd.proj[3]()
    fwd.two[4]()
    fwd.total[0]()
    turn_weights(0)
    fwd.total[1]()
    fwd.proj[6]()
    fwd.proj[5]()
    fwd.two[3]()
    fwd.total[2]()
    saved_probs(1)
    bwd.proj[1]()
    bwd.pz2()
    fwd.two[6]()
    fwd.total[4]()
    bwd.pzl()
    bwd.pz3()
    fwd.two[5]()
    turn_weights(2)
    bwd.pzs()
    saved_probs(3)
    bwd.proj[2]()
    fwd.total[6]()
    bwd.two[1]()
    saved_probs(0)
    bwd.pfa()
    fwd.total[3]()
    bwd.two[0]()
    fwd.total[5]()
    forward_head(6)
    bwd.pr()
    bwd.two[2]()
    bwd.pl2()
    forward_head(4)
    bwd.pfb()
    forward_head(3)
    forward_head(5)
    fwd.on[6]()
    bwd.proj[3]()
    forward_head(1)
    fwd.on[4]()
    forward_head(2)
    bwd.proj[4]()
    fwd.on[5]()
    fwd.back[6]()
    bwd.two[3]()
    bwd.total[2]()
    bwd.total[0]()
    forward_head(0)
    fwd.on[3]()
    bwd.total[1]()
    backward_rows(2)
    fwd.back[4]()
    bwd.two[4]()
    fwd.back[5]()
    fwd.on[1]()
    backward_rows(0)
    backward_rows(1)
    bwd.total[3]()
    fwd.a5()
    fwd.on[2]()
    backward_rows(3)
    bwd.total[4]()
    backward_rows(4)
    backward_end()
    fwd.back[1]()
    fwd.back[3]()
    fwd.a6()
    heads_out(fb, 6)
    fwd.a1b()
    heads_out(fb, 5)
    turn_weights(1)
    fwd.back[2]()
    queries_on(4)
    fwd.a2()
    bwd.on[6]()
    heads_out(fb, 4)
    fwd.a1()
    fwd.a2b()
    fwd.a3b()
    bwd.on[5]()
    queries_on(3)
    bwd.back[6]()
    fwd.on[0]()
    bwd.on[4]()
    queries_on(2)
    heads_out(fb, 2)
    heads_out(fb, 3)
    bwd.back[5]()
    fwd.back[0]()
    heads_out(fb, 0)
    fwd.finA()
    bwd.back[4]()
    heads_out(fb, 1)
    bwd.a5()
    queries_on(1)
    bwd.on[2]()
    bwd.on[3]()
    bwd.a6()
    fwd.finB()
    bwd.on[1]()
    bwd.back[2]()
    bwd.a1()
    bwd.a2()
    bwd.back[3]()
    queries_on(0)
    bwd.back[1]()
    bwd.a1b()
    bwd.on[0]()
    bwd.a3b()
    bwd.a2b()
    bwd.back[0]()
    bwd.finA()
    bwd.finB()
    got(*fb.hops, *ff.hops)
    drain(len(pending))
    assert count[0] == N_SEMS, count


def hand_over(a, b, a_out, b_out):
    a_out[...] = a[...]
    b_out[...] = b[...]


def per_device(fwd_input, grad_out, w_qkv, w_out, saved_qkv, rand_blocks):
    def vmem(*shape, dtype=BF16):
        return pltpu.VMEM(shape, dtype)

    def pair(rows, width_b, width_f):
        return [vmem(rows, width_b), vmem(rows, width_f)]

    any_space = pl.BlockSpec(memory_space=pl.ANY)
    fwd_next, grad_prev = pl.pallas_call(
        kernel,
        out_shape=[jax.ShapeDtypeStruct((TB, W), BF16)] * 2,
        in_specs=[any_space] * 5 + [pl.BlockSpec(memory_space=pltpu.SMEM)],
        out_specs=[any_space] * 2,
        scratch_shapes=[
            *pair(T, W, W), vmem(12 * W, HD), vmem(W, W), vmem(512, W), vmem(3, T, HD),
            vmem(16, 8, T, dtype=F32), vmem(T, T), vmem(T, HD),
            *pair(T, 512, 1536), *pair(512, 128, 384), *pair(512, 128, 384), *pair(T, 128, 384), *pair(T, 128, 384),
            *pair(T, 128, 384), vmem(T, HD, dtype=F32), vmem(T, HD, dtype=F32), vmem(T, 512), vmem(T, 1536),
            *pair(T, W, W), *pair(TB + LOW + 2 * (SIDE - CUT), W, W), *pair(2 * TB + 2 * CUT - MID + TB - SIDE, W, W),
            *pair(TB + CUT + MID + TB - SIDE, W, W), *pair(TB, W, W), vmem(512, 512), vmem(W, W),
            pltpu.SemaphoreType.DMA((24,)), pltpu.SemaphoreType.DMA((N_SENT,)), pltpu.SemaphoreType.DMA((N_SEMS,)),
        ],
        compiler_params=pltpu.CompilerParams(
            collective_id=0, has_side_effects=True, vmem_limit_bytes=62 * 1024 * 1024
        ),
        cost_estimate=pl.CostEstimate(flops=16_000_000_000, bytes_accessed=10_000_000, transcendentals=2_000_000),
    )(
        fwd_input.reshape(TB, W),
        grad_out.reshape(TB, W),
        w_qkv.reshape(12 * W, HD),
        w_out.reshape(512, W),
        saved_qkv.reshape(3, T, HD),
        rand_blocks.transpose(0, 3, 1, 2).reshape(3, 1, 16),
    )
    block = pl.BlockSpec((TB // 2, W), lambda i: (i, 0))
    fwd_next, grad_prev = pl.pallas_call(
        hand_over,
        grid=(2,),
        out_shape=[jax.ShapeDtypeStruct((TB, W), BF16)] * 2,
        in_specs=[block] * 2,
        out_specs=[block] * 2,
    )(fwd_next, grad_prev)
    return (fwd_next[None], grad_prev[None])


def solution(mesh):
    placed = (
        P("section", "ctx", "tp"),
        P("section", "ctx", "tp"),
        P("section", None, "tp", "ctx", None),
        P("section", "ctx", None, "tp"),
        P("section", None, None, ("ctx", "tp"), None),
        P("section", ("ctx", "tp"), None, None),
    )
    return jax.shard_map(
        per_device,
        mesh=mesh,
        in_specs=placed,
        out_specs=(P("section", "ctx", "tp"), P("section", "ctx", "tp")),
        check_vma=False,
    )
```

```python
import functools
import math
import types

import jax
import jax.numpy as jnp
from jax import lax
from jax.experimental import pallas as pl
from jax.experimental.pallas import tpu as pltpu
from jax.sharding import PartitionSpec as P

MESH = pl.DeviceIdType.MESH
F32, BF16 = jnp.float32, jnp.bfloat16
T, TB, W, HD = 1024, 128, 1536, 128
PLACES = ((0, 0), (0, 1), (-1, 0), (1, 0), (-1, 1), (1, 1), (2, 0), (2, 1))
ORDER = (
    (0, 0), (0, 1), (2, 1), (3, 1), (1, 0), (2, 0), (3, 0), (1, 1),
    (6, 1), (4, 1), (4, 0), (5, 0), (5, 1), (6, 0), (7, 0), (7, 1),
)
ROW = {block: 64 * i for i, block in enumerate(ORDER)}
GROUPS = (
    ((0, 2), (2, 3), (5, 3), (8, 4), (12, 4)),
    ((0, 2), (2, 3), (5, 3), (8, 2), (10, 2), (12, 2), (14, 2)),
)
RESULTS = ((0, 2), (2, 2), (4, 3), (7, 1), (8, 4), (12, 2), (14, 2))
CUT, MID, SIDE = 64, 96, 112
LOW = TB - CUT
N_SENT, N_SEMS = 64, 198


def nn(a, b):
    return lax.dot_general(a, b, (((1,), (0,)), ((), ())), preferred_element_type=F32)


def nt(a, b):
    return lax.dot_general(a, b, (((1,), (1,)), ((), ())), preferred_element_type=F32)


def tn(a, b):
    return lax.dot_general(a, b, (((0,), (0,)), ((), ())), preferred_element_type=F32)


def kernel(fin, gout, wq, wo_in, sv_in, rnd, fnext, gprev, x_b, x_f, w_raw, wp, wo, sv, bias, probs, head_out,
           yp_b, yp_f, y2u_b, y2u_f, y2d_b, y2d_f, ya_b, ya_f, yb_b, yb_f, act_b, act_f, dk, dv, mixed, grads,
           xs_b, xs_f, rz_b, rz_f, rl_b, rl_f, rr_b, rr_f, out_b, out_f, pick, wpt, load_sem, send_sem, recv_sem):
    sec, ctx, tp = lax.axis_index("section"), lax.axis_index("ctx"), lax.axis_index("tp")
    zl, xc = ctx // 4, ctx % 4

    def at_place(dx, dz):
        return (zl + dz) % 2 * 4 + (xc + dx + 4) % 4

    owner = [at_place(*place) for place in PLACES]
    right, left, across = {"ctx": owner[3]}, {"ctx": owner[2]}, {"ctx": owner[1]}
    up, down = {"tp": (tp + 1) % 4}, {"tp": (tp + 3) % 4}
    sections = lax.axis_size("section")
    after, before = {"section": (sec + 1) % sections}, {"section": (sec + sections - 1) % sections}
    scale = 1.0 / math.sqrt(HD)

    loads = []

    def load(src, dst):
        copy = pltpu.make_async_copy(src, dst, load_sem.at[len(loads)])
        loads.append(copy)
        copy.start()
        return copy

    sv_loads = [
        load(
            sv_in.at[:, pl.ds(pl.multiple_of(owner[s] * TB + half * 64, 64), 64), :],
            sv.at[:, pl.ds(ROW[s, half], 64), :],
        )
        for s, half in ORDER
    ]
    own_loads = [load(gout, x_b.at[pl.ds(0, TB)]), load(fin, x_f.at[pl.ds(0, TB)])]
    wo_loads = [
        load(wo_in.at[pl.ds(pl.multiple_of((tp + j) % 4 * HD, HD), HD), :], wo.at[pl.ds(j * HD, HD), :])
        for j in range(4)
    ]
    wq_loads = [load(wq, w_raw)]

    barrier = pltpu.get_barrier_semaphore()
    for other in (right, left, across, up, down, after, before):
        pl.semaphore_signal(barrier, inc=1, device_id=other, device_id_type=MESH)
    pl.semaphore_wait(barrier, 7)

    count, pending, free = [0], [], list(range(N_SENT))

    class Message:
        def __init__(self, src, dst, other):
            self.ends = (src, dst, other)
            self.k = count[0]
            count[0] += 1

        def copy(self, slot):
            src, dst, other = self.ends
            return pltpu.make_async_remote_copy(
                src_ref=src, dst_ref=dst, send_sem=send_sem.at[slot], recv_sem=recv_sem.at[self.k],
                device_id=other, device_id_type=MESH,
            )

    def msg(src, dst, other):
        return Message(src, dst, other)

    def row(s, lo):
        return ROW[s, lo // CUT] + lo % CUT

    def part(ref, s, lo, hi):
        return ref.at[pl.ds(row(s, lo), hi - lo)]

    class Flow:
        pass

    flows = []
    for own, x, yp, y2u, y2d, ya, yb, act, heads, xs, rz, rl, rr, out, dest, hop, w in (
        (gout, x_b, yp_b, y2u_b, y2d_b, ya_b, yb_b, act_b, grads, xs_b, rz_b, rl_b, rr_b, out_b, gprev, before, 128),
        (fin, x_f, yp_f, y2u_f, y2d_f, ya_f, yb_f, act_f, mixed, xs_f, rz_f, rl_f, rr_f, out_f, fnext, after, 384),
    ):
        f = Flow()
        f.x, f.yp, f.y2u, f.y2d, f.ya, f.yb, f.act, f.heads = x, yp, y2u, y2d, ya, yb, act, heads
        f.xs, f.out, f.w = xs, out, w
        own_part = {0: own.at[pl.ds(0, CUT)], CUT: own.at[pl.ds(CUT, LOW)]}

        def both(s, other):
            return [msg(own_part[lo], part(x, s, lo, hi), other) for lo, hi in ((0, CUT), (CUT, TB))]

        f.own_r, f.own_l, f.own_z = both(2, right), both(3, left), both(1, across)
        f.fwd_r = msg(part(x, 2, 0, CUT), part(x, 6, 0, CUT), right)
        f.fwd_rq = msg(part(x, 2, CUT, MID), part(x, 6, CUT, MID), right)
        f.fwd_l = msg(part(x, 3, MID, TB), part(x, 6, MID, TB), left)
        f.fwd_z2 = msg(part(x, 2, CUT, SIDE), part(x, 4, CUT, SIDE), across)
        f.fwd_z3 = msg(part(x, 3, CUT, SIDE), part(x, 5, CUT, SIDE), across)
        f.z_r = msg(part(x, 1, 0, CUT), part(x, 4, 0, CUT), right)
        f.z_l = msg(part(x, 1, 0, CUT), part(x, 5, 0, CUT), left)
        f.z_rq = msg(part(x, 1, SIDE, TB), part(x, 4, SIDE, TB), right)
        f.z_lq = msg(part(x, 1, SIDE, TB), part(x, 5, SIDE, TB), left)
        f.z_l2 = msg(part(x, 5, 0, CUT), part(x, 7, 0, CUT), left)
        f.far_a = msg(part(x, 6, CUT, MID), part(x, 7, CUT, MID), across)
        f.far_b = msg(part(x, 6, MID, TB), part(x, 7, MID, TB), across)
        f.s2u, f.s2d, f.s1u, f.s1d = [], [], [], []
        f.groups = GROUPS[w == 384]
        for at, n in f.groups:
            all_rows, half = pl.ds(at * 64, n * 64), pl.ds(at * 32, n * 32)
            first, last = pl.ds(at * 64, n * 32), pl.ds(at * 64 + n * 32, n * 32)
            f.s2u.append(msg(yp.at[first, pl.ds(2 * w, w)], y2u.at[half], up))
            f.s2d.append(msg(yp.at[last, pl.ds(2 * w, w)], y2d.at[half], down))
            f.s1u.append(msg(yp.at[all_rows, pl.ds(w, w)], ya.at[all_rows], up))
            f.s1d.append(msg(yp.at[all_rows, pl.ds(3 * w, w)], yb.at[all_rows], down))

        def round_y(groups, at_col, v):
            hu, hd, h2u, h2d = [], [], [], []
            for at, n in groups:
                all_rows = pl.ds(at * 64, n * 64)
                first, last = pl.ds(at * 64, n * 32), pl.ds(at * 64 + n * 32, n * 32)
                c = [pl.ds(heads.shape[1] // 4 * j + at_col, v) for j in range(4)]
                hu.append(msg(heads.at[all_rows, c[0]], heads.at[all_rows, c[3]], up))
                hd.append(msg(heads.at[all_rows, c[0]], heads.at[all_rows, c[1]], down))
                h2u.append(msg(heads.at[first, c[3]], heads.at[first, c[2]], up))
                h2d.append(msg(heads.at[last, c[1]], heads.at[last, c[2]], down))
            return hu, hd, h2u, h2d

        if w == 384:
            f.results = round_y(RESULTS, 0, HD)
        else:
            f.results = round_y(RESULTS, HD, 2 * HD)
            f.queries = round_y(f.groups, 0, HD)
        def cuts(ref, *sizes):
            at = [sum(sizes[:i]) for i in range(len(sizes))]
            return [ref.at[pl.ds(lo, n)] for lo, n in zip(at, sizes)]

        f.zb6, f.zb2, f.zb3, f.z0a, f.z0b = cuts(rz, LOW, SIDE - CUT, SIDE - CUT, CUT, LOW)
        f.la5, f.la1, f.l3, f.l0a, f.l0b, f.lb1 = cuts(rl, CUT, CUT, TB - MID, CUT, LOW, TB - SIDE)
        f.ra1, f.r2a, f.r2q, f.r0a, f.r0b, f.rb1 = cuts(rr, CUT, CUT, MID - CUT, CUT, LOW, TB - SIDE)
        f.t7r, f.t7z = msg(part(xs, 7, 0, CUT), f.la5, right), msg(part(xs, 7, CUT, TB), f.zb6, across)
        f.t6l, f.t6q = msg(part(xs, 6, 0, CUT), f.r2a, left), msg(part(xs, 6, CUT, MID), f.r2q, left)
        f.t6r = msg(part(xs, 6, MID, TB), f.l3, right)
        f.t5r, f.t5z = msg(part(xs, 5, 0, CUT), f.la1, right), msg(part(xs, 5, CUT, SIDE), f.zb3, across)
        f.t4l, f.t4z = msg(part(xs, 4, 0, CUT), f.ra1, left), msg(part(xs, 4, CUT, SIDE), f.zb2, across)
        f.t5q, f.t4q = msg(part(xs, 5, SIDE, TB), f.lb1, right), msg(part(xs, 4, SIDE, TB), f.rb1, left)
        f.t3a, f.t3b = msg(part(xs, 3, 0, CUT), f.l0a, right), msg(part(xs, 3, CUT, TB), f.l0b, right)
        f.t2a, f.t2b = msg(part(xs, 2, 0, CUT), f.r0a, left), msg(part(xs, 2, CUT, TB), f.r0b, left)
        f.t1a, f.t1b = msg(part(xs, 1, 0, CUT), f.z0a, across), msg(part(xs, 1, CUT, TB), f.z0b, across)
        f.hops = [msg(out.at[r], dest.at[r], hop) for r in (pl.ds(0, CUT), pl.ds(CUT, LOW))]
        flows.append(f)
    fb, ff = flows

    def drain(n):
        for copy, slot in pending[:n]:
            copy.wait_send()
            free.append(slot)
        del pending[:n]

    def start(*messages):
        for message in messages:
            if not free:
                drain(8)
            slot = free.pop(0)
            copy = message.copy(slot)
            copy.start()
            pending.append((copy, slot))

    seen = set()

    def got(*messages):
        for message in messages:
            if message.k not in seen:
                seen.add(message.k)
                message.copy(0).wait_recv()

    def need(copies):
        while copies:
            copies.pop().wait()

    def here(f, block):
        s, half = block
        return {
            (0, 0): (), (0, 1): (), (1, 0): (f.own_z[0],), (1, 1): (f.own_z[1],), (2, 0): (f.own_r[0],),
            (2, 1): (f.own_r[1],), (3, 0): (f.own_l[0],), (3, 1): (f.own_l[1],), (4, 0): (f.z_r,), (4, 1): (f.fwd_z2, f.z_rq),
            (5, 0): (f.z_l,), (5, 1): (f.fwd_z3, f.z_lq), (6, 0): (f.fwd_r,), (6, 1): (f.fwd_rq, f.fwd_l), (7, 0): (f.z_l2,),
            (7, 1): (f.far_a, f.far_b),
        }[block]

    def pass_on(arrived, *onward):
        def step():
            got(*arrived)
            start(*onward)

        return step

    def add_into(dst, lo, n, srcs, cols=None):
        @pl.loop(0, n // 16, unroll=n // 16 if n <= 64 else 1)
        def _(i):
            r = pl.ds(lo + pl.multiple_of(i * 16, 16), 16)
            c = slice(None) if cols is None else cols
            total = dst[r, c].astype(F32)
            for src in srcs:
                total = total + src[pl.ds(pl.multiple_of(i * 16, 16), 16), :].astype(F32)
            dst[r, c] = total.astype(BF16)

    def rows_of(f, g):
        return pl.ds(f.groups[g][0] * 64, f.groups[g][1] * 64)

    def project(f, g):
        at, n = f.groups[g]
        for block in ORDER[at:at + n]:
            got(*here(f, block))
        need(own_loads)
        need(wo_loads)
        r = rows_of(f, g)

        @pl.loop(0, 4 * f.w // 256, unroll=4 * f.w // 256)
        def _(n):
            c = pl.ds(pl.multiple_of(n * 256, 256), 256)
            p = nn(f.x[r, :], wp[:, c]) if f is ff else nt(f.x[r, :], wo[c, :])
            f.yp[r, c] = p.astype(BF16)

        start(f.s2u[g], f.s2d[g])

    def sum_two(f, g):
        at, n = f.groups[g][0] * 64, f.groups[g][1] * 32
        got(f.s2u[g])
        add_into(f.yp, at, n, [f.y2u.at[pl.ds(at // 2, n)]], pl.ds(f.w, f.w))
        start(f.s1u[g])
        got(f.s2d[g])
        add_into(f.yp, at + n, n, [f.y2d.at[pl.ds(at // 2, n)]], pl.ds(3 * f.w, f.w))
        start(f.s1d[g])

    def sum_all(f, g):
        got(f.s1u[g], f.s1d[g])

        @pl.loop(0, f.groups[g][1] * 4)
        def _(i):
            r = pl.ds(f.groups[g][0] * 64 + pl.multiple_of(i * 16, 16), 16)
            total = f.yp[r, pl.ds(0, f.w)].astype(F32) + f.ya[r, :].astype(F32) + f.yb[r, :].astype(F32)
            f.act[r, :] = total.astype(BF16)

    def make_bias():
        lane = lax.broadcasted_iota(jnp.int32, (8, T), 1)
        lane_block = lane // 64
        key = jnp.zeros((8, T), jnp.int32)
        for i, (s, half) in enumerate(ORDER):
            key = jnp.where(lane_block == i, 2 * owner[s] + half, key)
        for i, (s, half) in enumerate(ORDER):
            q = 2 * owner[s] + half
            ok = (key < 2) | (key == q) | (key == (q + 1) % 16) | (key == (q + 15) % 16)
            for n in range(3):
                ok = ok | (key == rnd[n, 0, q])
            ok = ok | (jnp.full((8, T), q, jnp.int32) < 2)
            bias[i] = jnp.where(ok, 0.0, -1e30).astype(F32)

    def softmax(q, k, b0):
        n = q.shape[0] // 64
        s = nt(q, k).reshape(n, 8, 8, T) * scale + bias[pl.ds(b0, n)].reshape(n, 1, 8, T)
        s = s.reshape(n * 64, T)
        e = jnp.exp(s - jnp.max(s, axis=-1, keepdims=True))
        return (e * (1.0 / jnp.sum(e, axis=-1, keepdims=True))).astype(BF16)

    def saved_probs(quarter):
        need(sv_loads)

        @pl.loop(quarter * 2, quarter * 2 + 2)
        def _(i):
            r = pl.ds(pl.multiple_of(i * 128, 128), 128)
            p = softmax(sv[0, r, :], sv[1], i * 2)
            probs[r, :] = p
            head_out[r, :] = nn(p, sv[2]).astype(BF16)

    begun = []

    def backward_rows(g):
        if not begun:
            begun.append(g)
            dk[...] = jnp.zeros_like(dk)
            dv[...] = jnp.zeros_like(dv)
        r = rows_of(fb, g)
        grad = act_b[r, :]
        delta = jnp.sum(grad.astype(F32) * head_out[r, :].astype(F32), axis=-1, keepdims=True)
        p = probs[r, :]
        ds = (p.astype(F32) * (nt(grad, sv[2]) - delta)).astype(BF16)
        grads[r, pl.ds(0, HD)] = (nn(ds, sv[1]) * scale).astype(BF16)
        start(fb.queries[0][g], fb.queries[1][g])
        dk[...] += tn(ds, sv[0, r, :])
        dv[...] += tn(p, grad)

    def queries_on(g):
        got(fb.queries[0][g])
        start(fb.queries[2][g])
        got(fb.queries[1][g])
        start(fb.queries[3][g])

    def backward_end():
        grads[:, pl.ds(HD, HD)] = (dk[...] * scale).astype(BF16)
        grads[:, pl.ds(2 * HD, HD)] = dv[...].astype(BF16)

    def forward_head(g):
        at, n = RESULTS[g]
        size = 128 if n % 2 == 0 else n * 64

        @pl.loop(0, n * 64 // size)
        def _(i):
            r = pl.ds(at * 64 + pl.multiple_of(i * size, 64), size)
            p = softmax(act_f[r, pl.ds(0, HD)], act_f[:, pl.ds(HD, HD)], at + i * (size // 64))
            mixed[r, pl.ds(0, HD)] = nn(p, act_f[:, pl.ds(2 * HD, HD)]).astype(BF16)

        start(ff.results[0][g], ff.results[1][g])

    def heads_out(f, g):
        start(f.results[0][g], f.results[1][g])

    def heads_on(f, g):
        got(f.results[0][g])
        start(f.results[2][g])
        got(f.results[1][g])
        start(f.results[3][g])

    def order_weights():
        need(wq_loads)
        row, col = lax.broadcasted_iota(jnp.int32, (256, 256), 0), lax.broadcasted_iota(jnp.int32, (256, 256), 1)
        pick = jnp.where(col == row % 64 * 4 + (row // 64 + tp) % 4, 1.0, 0.0).astype(BF16)
        for c in range(3):
            @pl.loop(0, 12, unroll=6)
            def _(i):
                a = w_raw[pl.ds(pl.multiple_of((c * 24 + i * 2) * 256, 256), 256), :]
                b = w_raw[pl.ds(pl.multiple_of((c * 24 + i * 2 + 1) * 256, 256), 256), :]
                o = nn(pick, jnp.concatenate([a, b], axis=1)).astype(BF16)
                for j in range(4):
                    for k in range(2):
                        wp[pl.ds(pl.multiple_of(i * 128, 128) + k * 64, 64), pl.ds(j * 384 + c * HD, HD)] = (
                            o[j * 64:j * 64 + 64, k * HD:k * HD + HD]
                        )

    turned = []

    def turn_weights(c):
        if not turned:
            turned.append(c)
            row_id, col_id = (lax.broadcasted_iota(jnp.int32, (512, 512), k) for k in (0, 1))
            pick[...] = jnp.where(row_id == col_id % 128 * 4 + (col_id // 128 + tp) % 4, 1.0, 0.0).astype(BF16)

        @pl.loop(0, 12, unroll=3)
        def _(i):
            o = tn(w_raw[pl.ds(pl.multiple_of((c * 12 + i) * 512, 512), 512), :], pick[...]).astype(BF16)
            for j in range(4):
                wpt[pl.ds(j * 384 + c * HD, HD), pl.ds(pl.multiple_of(i * 128, 128), 128)] = o[:, j * HD:j * HD + HD]

    def project_back(f, g):
        got(f.results[2][g], f.results[3][g])
        if f is fb:
            at, n = RESULTS[g]
            for k, (first, number) in enumerate(fb.groups):
                if first < at + n and at < first + number:
                    got(fb.queries[2][k], fb.queries[3][k])
        r = pl.ds(RESULTS[g][0] * 64, RESULTS[g][1] * 64)

        @pl.loop(0, 6, unroll=6)
        def _(n):
            c = pl.ds(pl.multiple_of(n * 256, 256), 256)
            p = nn(f.heads[r, :], wo[:, c]) if f is ff else nn(f.heads[r, :], wpt[:, c])
            f.xs[r, c] = p.astype(BF16)

    def back(f, g):
        project_back(f, g)
        start(*{6: (f.t7z, f.t7r), 5: (f.t5z, f.t6l, f.t5q), 4: (f.t4z, f.t4l, f.t4q), 2: (f.t3a,)}.get(g, ()))

    def combine(f, arrived, adds, *onward):
        def step():
            got(*arrived)
            for at, n, srcs in adds:
                add_into(f.xs, at, n, srcs)
            start(*onward)

        return step

    def finish(f, lo, n, srcs, hop):
        @pl.loop(0, n // 16, unroll=n // 16 if n <= 64 else 1)
        def _(i):
            at = pl.multiple_of(i * 16, 16)
            r = pl.ds(lo + at, 16)
            total = f.xs[r, :].astype(F32) + f.x[r, :].astype(F32)
            for src in srcs:
                total = total + src[pl.ds(at, 16), :].astype(F32)
            f.out[r, :] = total.astype(BF16)

        start(hop)

    def finish_high(f):
        got(f.t3a, f.t2a, f.t1a)
        finish(f, 0, CUT, (f.l0a, f.r0a, f.z0a), f.hops[0])

    def finish_low(f):
        got(f.t3b, f.t2b, f.t1b)
        finish(f, CUT, LOW, (f.l0b, f.r0b, f.z0b), f.hops[1])

    for f in flows:
        f.do = types.SimpleNamespace(
            own1=pass_on((), f.own_z[0], f.own_r[1], f.own_l[1]),
            own2=pass_on((), f.own_z[1], f.own_r[0], f.own_l[0]),
            pz2=pass_on((f.own_r[1],), f.fwd_z2, f.fwd_rq),
            pz3=pass_on((f.own_l[1],), f.fwd_z3, f.fwd_l),
            pzl=pass_on((f.own_z[0],), f.z_l, f.z_r),
            pzs=pass_on((f.own_z[1],), f.z_rq, f.z_lq),
            pr=pass_on((f.own_r[0],), f.fwd_r),
            pfb=pass_on((f.fwd_l,), f.far_b),
            pfa=pass_on((f.fwd_rq,), f.far_a),
            pl2=pass_on((f.z_l,), f.z_l2),
            a6=combine(f, (f.t7z,), ((row(6, CUT), LOW, [f.zb6]),), f.t6q, f.t6r),
            a5=combine(f, (f.t7r,), ((row(5, 0), CUT, [f.la5]),), f.t5r),
            a2=combine(f, (f.t6l,), ((row(2, 0), CUT, [f.r2a]),), f.t2a),
            a1=combine(f, (f.t5r, f.t4l), ((row(1, 0), CUT, [f.la1, f.ra1]),), f.t1a),
            a1b=combine(f, (f.t5q, f.t4q), ((row(1, SIDE), TB - SIDE, [f.lb1, f.rb1]),), f.t1b),
            a3b=combine(
                f, (f.t5z, f.t6r), ((row(3, CUT), SIDE - CUT, [f.zb3]), (row(3, MID), TB - MID, [f.l3])), f.t3b
            ),
            a2b=combine(
                f, (f.t4z, f.t6q), ((row(2, CUT), SIDE - CUT, [f.zb2]), (row(2, CUT), MID - CUT, [f.r2q])), f.t2b
            ),
            finA=lambda f=f: finish_high(f),
            finB=lambda f=f: finish_low(f),
            proj=[functools.partial(project, f, g) for g in range(len(f.groups))],
            two=[functools.partial(sum_two, f, g) for g in range(len(f.groups))],
            total=[functools.partial(sum_all, f, g) for g in range(len(f.groups))],
            on=[functools.partial(heads_on, f, g) for g in range(len(RESULTS))],
            back=[functools.partial(back, f, g) for g in range(len(RESULTS))],
        )
    fwd, bwd = ff.do, fb.do

    fwd.own1()
    fwd.own2()
    order_weights()
    fwd.proj[0]()
    fwd.pzl()
    fwd.pz3()
    fwd.proj[1]()
    bwd.proj[0]()
    fwd.pz2()
    fwd.two[0]()
    fwd.proj[2]()
    fwd.pzs()
    fwd.two[1]()
    fwd.proj[4]()
    fwd.pr()
    make_bias()
    fwd.pl2()
    fwd.pfb()
    fwd.pfa()
    fwd.two[2]()
    bwd.own1()
    saved_probs(2)
    bwd.own2()
    fwd.proj[3]()
    fwd.two[4]()
    fwd.total[0]()
    turn_weights(0)
    fwd.total[1]()
    fwd.proj[6]()
    fwd.proj[5]()
    fwd.two[3]()
    fwd.total[2]()
    saved_probs(1)
    bwd.proj[1]()
    bwd.pz2()
    fwd.two[6]()
    fwd.total[4]()
    bwd.pzl()
    bwd.pz3()
    fwd.two[5]()
    turn_weights(2)
    bwd.pzs()
    saved_probs(3)
    bwd.proj[2]()
    fwd.total[6]()
    bwd.two[1]()
    saved_probs(0)
    bwd.pfa()
    fwd.total[3]()
    bwd.two[0]()
    fwd.total[5]()
    forward_head(6)
    bwd.pr()
    bwd.two[2]()
    bwd.pl2()
    forward_head(4)
    bwd.pfb()
    forward_head(3)
    forward_head(5)
    fwd.on[6]()
    bwd.proj[3]()
    forward_head(1)
    fwd.on[4]()
    forward_head(2)
    bwd.proj[4]()
    fwd.on[5]()
    fwd.back[6]()
    bwd.two[3]()
    bwd.total[2]()
    bwd.total[0]()
    forward_head(0)
    fwd.on[3]()
    bwd.total[1]()
    backward_rows(2)
    fwd.back[4]()
    bwd.two[4]()
    fwd.back[5]()
    fwd.on[1]()
    backward_rows(0)
    backward_rows(1)
    bwd.total[3]()
    fwd.a5()
    fwd.on[2]()
    backward_rows(3)
    bwd.total[4]()
    backward_rows(4)
    backward_end()
    fwd.back[1]()
    fwd.back[3]()
    fwd.a6()
    heads_out(fb, 6)
    fwd.a1b()
    heads_out(fb, 5)
    turn_weights(1)
    fwd.back[2]()
    queries_on(4)
    fwd.a2()
    bwd.on[6]()
    heads_out(fb, 4)
    fwd.a1()
    fwd.a2b()
    fwd.a3b()
    bwd.on[5]()
    queries_on(3)
    bwd.back[6]()
    fwd.on[0]()
    bwd.on[4]()
    queries_on(2)
    heads_out(fb, 2)
    heads_out(fb, 3)
    bwd.back[5]()
    fwd.back[0]()
    heads_out(fb, 0)
    fwd.finA()
    bwd.back[4]()
    heads_out(fb, 1)
    bwd.a5()
    queries_on(1)
    bwd.on[2]()
    bwd.on[3]()
    bwd.a6()
    fwd.finB()
    bwd.on[1]()
    bwd.back[2]()
    bwd.a1()
    bwd.a2()
    bwd.back[3]()
    queries_on(0)
    bwd.back[1]()
    bwd.a1b()
    bwd.on[0]()
    bwd.a3b()
    bwd.a2b()
    bwd.back[0]()
    bwd.finA()
    bwd.finB()
    got(*fb.hops, *ff.hops)
    drain(len(pending))
    assert count[0] == N_SEMS, count


def hand_over(a, b, a_out, b_out):
    a_out[...] = a[...]
    b_out[...] = b[...]


def per_device(fwd_input, grad_out, w_qkv, w_out, saved_qkv, rand_blocks):
    def vmem(*shape, dtype=BF16):
        return pltpu.VMEM(shape, dtype)

    def pair(rows, width_b, width_f):
        return [vmem(rows, width_b), vmem(rows, width_f)]

    any_space = pl.BlockSpec(memory_space=pl.ANY)
    fwd_next, grad_prev = pl.pallas_call(
        kernel,
        out_shape=[jax.ShapeDtypeStruct((TB, W), BF16)] * 2,
        in_specs=[any_space] * 5 + [pl.BlockSpec(memory_space=pltpu.SMEM)],
        out_specs=[any_space] * 2,
        scratch_shapes=[
            *pair(T, W, W), vmem(12 * W, HD), vmem(W, W), vmem(512, W), vmem(3, T, HD),
            vmem(16, 8, T, dtype=F32), vmem(T, T), vmem(T, HD),
            *pair(T, 512, 1536), *pair(512, 128, 384), *pair(512, 128, 384), *pair(T, 128, 384), *pair(T, 128, 384),
            *pair(T, 128, 384), vmem(T, HD, dtype=F32), vmem(T, HD, dtype=F32), vmem(T, 512), vmem(T, 1536),
            *pair(T, W, W), *pair(TB + LOW + 2 * (SIDE - CUT), W, W), *pair(2 * TB + 2 * CUT - MID + TB - SIDE, W, W),
            *pair(TB + CUT + MID + TB - SIDE, W, W), *pair(TB, W, W), vmem(512, 512), vmem(W, W),
            pltpu.SemaphoreType.DMA((24,)), pltpu.SemaphoreType.DMA((N_SENT,)), pltpu.SemaphoreType.DMA((N_SEMS,)),
        ],
        compiler_params=pltpu.CompilerParams(
            collective_id=0, has_side_effects=True, vmem_limit_bytes=62 * 1024 * 1024
        ),
        cost_estimate=pl.CostEstimate(flops=16_000_000_000, bytes_accessed=10_000_000, transcendentals=2_000_000),
    )(
        fwd_input.reshape(TB, W),
        grad_out.reshape(TB, W),
        w_qkv.reshape(12 * W, HD),
        w_out.reshape(512, W),
        saved_qkv.reshape(3, T, HD),
        rand_blocks.transpose(0, 3, 1, 2).reshape(3, 1, 16),
    )
    block = pl.BlockSpec((TB // 2, W), lambda i: (i, 0))
    fwd_next, grad_prev = pl.pallas_call(
        hand_over,
        grid=(2,),
        out_shape=[jax.ShapeDtypeStruct((TB, W), BF16)] * 2,
        in_specs=[block] * 2,
        out_specs=[block] * 2,
    )(fwd_next, grad_prev)
    return (fwd_next[None], grad_prev[None])


def solution(mesh):
    placed = (
        P("section", "ctx", "tp"),
        P("section", "ctx", "tp"),
        P("section", None, "tp", "ctx", None),
        P("section", "ctx", None, "tp"),
        P("section", None, None, ("ctx", "tp"), None),
        P("section", ("ctx", "tp"), None, None),
    )
    return jax.shard_map(
        per_device,
        mesh=mesh,
        in_specs=placed,
        out_specs=(P("section", "ctx", "tp"), P("section", "ctx", "tp")),
        check_vma=False,
    )
```
